256 devices in a mesh: bit: 32 (over y, z), sect: 8 (over x, core).
Axes of the slice: x: 4, y: 4, z: 8, core: 2. Of those that a mesh axis runs over, the one named last changes fastest.
Arguments:
- positions: float32 [3, 8192, 128], P(None, ('bit', 'sect')), as said below
- strengths: float32 [3, 8192, 128], P(None, ('bit', 'sect')), may hold values from -1 to 1
- cores: float32 [8192, 128], P(('bit', 'sect')), may hold values from 0.1 to 0.4
- far_coef: float32 [12, 8192], P(None, ('bit', 'sect')), may hold values from -4 to 4
- near_list: int32 [8192, 8], P(('bit', 'sect')), may hold values from 0 to 8191, as said below
- near_count: int32 [8192], P(('bit', 'sect')), may hold values from 1 to 8, as said below
Outputs:
- velocity: float32 [3, 8192, 128], P(None, ('bit', 'sect'))
- stretching: float32 [3, 8192, 128], P(None, ('bit', 'sect'))
The draws below stay inside these ranges and needn't reach their ends.
Inputs may be any that keep to these rules, and one draw needn't show every extreme that they name: `positions`: each leaf's particles lie in a cube of side one of its own (the leaf's cell), at integer corners; the cells of one device form a block, and the cells of leaves that one leaf lists are its own or touch it. `near_list`: leaf g lies on the device of flat index g // 32 (bit index times the size of sect plus sect index). Slot 0 of a leaf's list is the leaf itself. Every other entry is a leaf of the same device, or one of the first 24 leaves of a device with the same bit index and a sect index one lower or one higher, or of a device with the same sect index whose bit index differs in exactly one bit. Entries may repeat. Only the first near_count[t] slots of leaf t's list are used; on every device some leaf uses all 8.
All inputs are finite; a program needn't handle non-finite values.
Results may differ from the reference program's by a relative error of at most 0.0003.
Values sent between devices are 32-bit elements; how exact they have to be, the bound alone decides.
No kernel may reach another device: no remote copies, remote signals or barrier semaphores. Data moves between devices by JAX's collectives and lax.ppermute only.
A program may use at most 64 MiB of HBM per device.

```python
import math
import jax
import jax.numpy as jnp
from jax import lax

PL = 128
LEAF_DEV = 32
NBR = 8
BND = 24
LEAVES = 8192
N_BIT = 32
N_SECT = 8


def grid_bits():
    levels = N_BIT.bit_length() - 1
    y_bits = levels // 2
    z_bits = levels - y_bits
    return (y_bits, z_bits)


def inverse_gray(gray_value):
    decoded = gray_value
    for amount in range(1, 8):
        decoded = jnp.bitwise_xor(decoded, jnp.right_shift(gray_value, amount))
    return decoded


def gray_code(plain_value):
    return jnp.bitwise_xor(plain_value, jnp.right_shift(plain_value, 1))


def layer_place(layer_index, layers):
    return jnp.where(layer_index == 0, 0, jnp.where(layer_index == 1, layers - 1, layer_index - 1))


def leaf_cells():
    y_bits, z_bits = grid_bits()
    layers = LEAF_DEV // 4
    leaf_index = jnp.arange(LEAVES, dtype=jnp.int32)
    device = leaf_index // LEAF_DEV
    local_index = leaf_index % LEAF_DEV
    bit_of = device // N_SECT
    sect_of = device % N_SECT
    layer_index = local_index // 4
    cell_x = sect_of * layers + layer_place(layer_index, layers)
    cell_y = inverse_gray(jnp.right_shift(bit_of, z_bits)) * 2 + local_index % 4 // 2
    cell_z = inverse_gray(jnp.bitwise_and(bit_of, (1 << z_bits) - 1)) * 2 + local_index % 2
    return (cell_x, cell_y, cell_z)


def draw_positions(key, part):
    key = jax.random.fold_in(key, 5)
    cell_x, cell_y, cell_z = leaf_cells()
    anchor = jnp.stack([cell_x, cell_y, cell_z]).astype(jnp.float32)[:, :, None]
    within_cell = jax.random.uniform(key, (3, LEAVES, PL), jnp.float32)
    return anchor + within_cell


def draw_near_list(key, part):
    key = jax.random.fold_in(key, 11)
    y_bits, z_bits = grid_bits()
    layers = LEAF_DEV // 4
    cell_x, cell_y, cell_z = leaf_cells()
    leaf_index = jnp.arange(LEAVES, dtype=jnp.int32)
    device = leaf_index // LEAF_DEV
    bit_of = (device // N_SECT)[:, None]
    sect_of = (device % N_SECT)[:, None]
    offsets = jax.random.randint(key, (3, LEAVES, NBR), -1, 2)
    near_x = cell_x[:, None] + offsets[0]
    near_y = cell_y[:, None] + offsets[1]
    near_z = cell_z[:, None] + offsets[2]
    extent_x = N_SECT * layers
    extent_y = 2 << y_bits
    extent_z = 2 << z_bits
    inside = (near_x >= 0) & (near_x < extent_x) & (near_y >= 0) & (near_y < extent_y) & (near_z >= 0) & (near_z < extent_z)
    near_x = jnp.clip(near_x, 0, extent_x - 1)
    near_y = jnp.clip(near_y, 0, extent_y - 1)
    near_z = jnp.clip(near_z, 0, extent_z - 1)
    sect_to = near_x // layers
    x_within = near_x % layers
    layer_to = jnp.where(x_within == 0, 0, jnp.where(x_within == layers - 1, 1, x_within + 1))
    bit_to = jnp.bitwise_or(jnp.left_shift(gray_code(near_y // 2), z_bits), gray_code(near_z // 2))
    local_to = layer_to * 4 + near_y % 2 * 2 + near_z % 2
    device_to = bit_to * N_SECT + sect_to
    chosen_leaf = device_to * LEAF_DEV + local_to
    differs = jnp.bitwise_xor(bit_to, bit_of)
    one_bit = (differs > 0) & (jnp.bitwise_and(differs, differs - 1) == 0)
    allowed = (device_to == device[:, None]) | (bit_to == bit_of) & (jnp.abs(sect_to - sect_of) == 1) & (local_to < BND) | (sect_to == sect_of) & one_bit & (local_to < BND)
    chosen_leaf = jnp.where(inside & allowed, chosen_leaf, leaf_index[:, None])
    chosen_leaf = chosen_leaf.at[:, 0].set(leaf_index)
    return chosen_leaf.astype(jnp.int32)


def draw_near_count(key, part):
    key = jax.random.fold_in(key, 23)
    key_parts = jax.random.split(key, 3)
    devices = LEAVES // LEAF_DEV
    base_count = jax.random.randint(key_parts[0], (LEAVES,), 1, NBR + 1)
    factor = jnp.repeat(jax.random.randint(key_parts[1], (devices,), 1, 5), LEAF_DEV)
    scaled = jnp.maximum(1, base_count * factor // 4)
    picked = jnp.repeat(jax.random.randint(key_parts[2], (devices,), 0, LEAF_DEV), LEAF_DEV)
    local_index = jnp.arange(LEAVES, dtype=jnp.int32) % LEAF_DEV
    return jnp.where(local_index == picked, NBR, scaled).astype(jnp.int32)


def block_levels(own_key, shape, cuts, low, high):
    factor_of, own = 1.0, jax.random.fold_in(own_key, 6)
    for position, blocks in cuts:
        draws = jnp.exp(jax.random.uniform(jax.random.fold_in(own, position), (blocks,), jnp.float32, low / len(cuts), high / len(cuts)))
        factor_of = factor_of * jnp.repeat(draws, shape[position] // blocks).reshape([-1 if axis == position else 1 for axis in range(len(shape))])
    return factor_of


def centred(stream_key, shape, scale, reach, pieces=(), held_as=jnp.bfloat16):
    factor_of = block_levels(stream_key, shape, pieces, -0.22, 0.18) if pieces else 1.0
    drawn = jax.random.normal(stream_key, shape, jnp.float32) * scale * factor_of
    return jnp.minimum(jnp.maximum(drawn, -reach), reach).astype(held_as)


def setup_inputs(seed: int = 0) -> dict:
    key_of = jax.random.split(jax.random.key(seed), 7)
    positions = draw_positions(jax.random.fold_in(key_of[6], 71), 0)
    strengths = centred(key_of[1], (3, LEAVES, PL), 0.15, 1.0, ((1, 256),), jnp.float32)
    cores = jnp.clip(0.1 + 0.3 * jax.random.uniform(key_of[2], (LEAVES, PL), jnp.float32) ** block_levels(key_of[2], (LEAVES, PL), ((0, 256),), -0.2, 0.2), 0.1, 0.4)
    far_coef = centred(key_of[3], (12, LEAVES), 1.0, 4.0, ((1, 256),), jnp.float32)
    near_list = draw_near_list(jax.random.fold_in(key_of[6], 71), 0)
    near_count = draw_near_count(jax.random.fold_in(key_of[6], 71), 0)
    return {"positions": positions, "strengths": strengths, "cores": cores, "far_coef": far_coef, "near_list": near_list, "near_count": near_count}


inv_four_pi = 1.0 / (4.0 * math.pi)

def pair_sums(target_pos, target_str, source, active):
    offset = [target_pos[member][:, :, None] - source[member][:, None, :] for member in range(3)]
    source_str = [source[3 + member][:, None, :] * active[:, None, None] for member in range(3)]
    radius = source[6][:, None, :]
    spread = offset[0] * offset[0] + offset[1] * offset[1] + offset[2] * offset[2] + radius * radius
    kernel = 1.0 / (spread * jnp.sqrt(spread))
    steeper = kernel / spread
    crossed = [offset[1] * source_str[2] - offset[2] * source_str[1], offset[2] * source_str[0] - offset[0] * source_str[2], offset[0] * source_str[1] - offset[1] * source_str[0]]
    target_cols = [target_str[member][:, :, None] for member in range(3)]
    projected = target_cols[0] * offset[0] + target_cols[1] * offset[1] + target_cols[2] * offset[2]
    twisted = [target_cols[1] * source_str[2] - target_cols[2] * source_str[1], target_cols[2] * source_str[0] - target_cols[0] * source_str[2], target_cols[0] * source_str[1] - target_cols[1] * source_str[0]]
    velo = jnp.stack([lax.optimization_barrier(jnp.sum(kernel * crossed[member], axis=-1)) for member in range(3)])
    stre = jnp.stack([lax.optimization_barrier(jnp.sum(kernel * twisted[member] - 3.0 * steeper * projected * crossed[member], axis=-1)) for member in range(3)])
    return (velo, stre)

def finish(target_pos, target_str, coefs, near_vel, near_str):
    centre = lax.optimization_barrier(jnp.mean(target_pos, axis=2, keepdims=True))
    offset = target_pos - centre
    velocity = []
    stretching = []
    for row in range(3):
        grad_row = [coefs[3 + 3 * row + col][:, None] for col in range(3)]
        velocity.append(-inv_four_pi * near_vel[row] + coefs[row][:, None] + grad_row[0] * offset[0] + grad_row[1] * offset[1] + grad_row[2] * offset[2])
        stretching.append(-inv_four_pi * near_str[row] + grad_row[0] * target_str[0] + grad_row[1] * target_str[1] + grad_row[2] * target_str[2])
    return (jnp.stack(velocity), jnp.stack(stretching))

def reference(positions, strengths, cores, far_coef, near_list, near_count):
    per_block = 64
    blocks = LEAVES // per_block

    def one_block(number):
        first = number * per_block
        target_pos = lax.dynamic_slice_in_dim(positions, first, per_block, 1)
        target_str = lax.dynamic_slice_in_dim(strengths, first, per_block, 1)
        lists = lax.dynamic_slice_in_dim(near_list, first, per_block, 0)
        counts = lax.dynamic_slice_in_dim(near_count, first, per_block, 0)
        coefs = lax.dynamic_slice_in_dim(far_coef, first, per_block, 1)

        def add_slot(slot, totals):
            chosen = lax.dynamic_index_in_dim(lists, slot, 1, keepdims=False).astype(jnp.int32)
            source = jnp.concatenate([jnp.take(positions, chosen, axis=1), jnp.take(strengths, chosen, axis=1), jnp.take(cores, chosen, axis=0)[None]], axis=0)
            active = (slot < counts).astype(jnp.float32)
            velo, stre = pair_sums(target_pos, target_str, source, active)
            return (totals[0] + velo, totals[1] + stre)
        zeros = jnp.zeros((3, per_block, PL), jnp.float32)
        near_vel, near_str = lax.fori_loop(0, NBR, add_slot, (zeros, zeros))
        return finish(target_pos, target_str, coefs, near_vel, near_str)
    velocity, stretching = lax.map(one_block, jnp.arange(blocks, dtype=jnp.int32))
    velocity = jnp.transpose(velocity, (1, 0, 2, 3)).reshape(3, LEAVES, PL)
    stretching = jnp.transpose(stretching, (1, 0, 2, 3)).reshape(3, LEAVES, PL)
    return (velocity, stretching)
```

```python
import math

import jax
import jax.numpy as jnp
from jax import lax
from jax.experimental import pallas as pl
from jax.experimental.pallas import tpu as pltpu
from jax.sharding import PartitionSpec as P

inv_four_pi = 1.0 / (4.0 * math.pi)
f32, bf16, i32 = jnp.float32, jnp.bfloat16, jnp.int32

LEAF = 32
PART = 128
SLOTS = 8
EDGE = 24
PAIRS = LEAF * SLOTS
BATCH = 16
ROOM = PAIRS + BATCH
TABLE = (LEAF + 1) * 32
SUMS = (LEAF + 1) * 16


def rounded(value):
    return value.astype(bf16).astype(f32)


def split3(value):
    high = rounded(value)
    rest = value - high
    mid = rounded(rest)
    return high, mid, rest - mid


def split2(value):
    high = value.astype(bf16)
    return high, (value - high.astype(f32)).astype(bf16)


def leaf_rows(pos, group):
    rows = pl.ds(group * 8, 8)
    point = [pos[k, rows, :] for k in range(3)]
    centre = [jnp.mean(v, axis=1, keepdims=True) for v in point]
    return point, centre, [v - c for v, c in zip(point, centre)]


def build_targets(pos, stren, centres, table):
    for group in range(LEAF // 8):
        _, centre, off = leaf_rows(pos, group)
        a = [stren[k, pl.ds(group * 8, 8), :] for k in range(3)]
        zero = jnp.zeros((8, PART), f32)
        one = jnp.ones((8, PART), f32)
        for k in range(8):
            row = jnp.broadcast_to(centre[k], (8, PART)) if k < 3 else zero
            centres[pl.ds(group * 64 + k, 8, stride=8), :] = row
        left = [split3(-2.0 * v) for v in off]
        right = [split3(-v) for v in a]
        square = split3(off[0] * off[0] + off[1] * off[1] + off[2] * off[2])
        along = split3(off[0] * a[0] + off[1] * a[1] + off[2] * a[2])
        rows = []
        for part in (0, 1, 2, 0, 1, 0):
            rows += [(left[k][part], right[k][part]) for k in range(3)]
        rows += [(one, zero)] * 3
        rows += [(square[k], along[k]) for k in range(3)]
        rows += [(zero, zero)] * 8
        for k, (spread_row, proj_row) in enumerate(rows):
            where = pl.ds(group * 256 + k, 8, stride=32)
            table[where, :] = spread_row
            table[pl.ds(TABLE + group * 256 + k, 8, stride=32), :] = proj_row


def source_rows(gathered, left, right, group):
    first = pl.multiple_of(group * 64, 64)
    q = [gathered[pl.ds(first + k, 8, stride=8), :] for k in range(7)]
    x, a, core = q[:3], q[3:6], q[6]
    part = [split3(v) for v in x]
    size = split3(x[0] * x[0] + x[1] * x[1] + x[2] * x[2] + core * core)
    one = jnp.ones((8, PART), f32)
    rows = []
    for level in (0, 0, 0, 1, 1, 2):
        rows += [part[k][level] for k in range(3)]
    rows += list(size) + [one] * 3
    base = pl.multiple_of(group * 192, 64)
    for k, row in enumerate(rows):
        left[pl.ds(base + k, 8, stride=24), :] = row
    crossed = [
        x[1] * a[2] - x[2] * a[1],
        x[2] * a[0] - x[0] * a[2],
        x[0] * a[1] - x[1] * a[0],
    ]
    base = pl.multiple_of(group * 128, 128)
    for k, row in enumerate(a + crossed):
        high = rounded(row)
        right[pl.ds(base + k, 8, stride=16), :] = high
        right[pl.ds(base + 6 + k, 8, stride=16), :] = row - high
    for k in range(12, 16):
        right[pl.ds(base + k, 8, stride=16), :] = jnp.zeros((8, PART), f32)


def pair_batch(step, target_of, table, left, right, acc):
    results = []
    pad = jnp.zeros((8, PART), f32)
    for lane in range(BATCH):
        pair = step * BATCH + lane
        target = target_of[pair]
        lhs = left[pl.ds(pl.multiple_of(pair * 24, 8), 24), :]
        lhs = jnp.concatenate([lhs, pad], axis=0).astype(bf16)
        first = pl.multiple_of(target * 32, 32)
        rhs = jnp.concatenate(
            [table[pl.ds(first, 32), :], table[pl.ds(TABLE + first, 32), :]], axis=1
        ).astype(bf16)
        both = lax.dot_general(lhs, rhs, (((0,), (0,)), ((), ())), preferred_element_type=f32)
        spread, proj = both[:, :PART], both[:, PART:]
        root = lax.rsqrt(spread)
        square = root * root
        kernel = root * square
        weight = kernel * square * proj
        k_high, k_low = split2(kernel)
        w_high, w_low = split2(weight)
        pairs = jnp.concatenate(
            [jnp.concatenate([k_high, w_high], axis=1), jnp.concatenate([k_low, w_low], axis=1)], axis=0
        )
        rows = right[pl.ds(pl.multiple_of(pair * 16, 16), 16), :].astype(bf16)
        rows = jnp.concatenate([rows, rows], axis=1)
        results.append((target, jnp.dot(rows, pairs, preferred_element_type=f32)))
    for target, value in results:
        first = pl.multiple_of(target * 16, 16)
        for side in range(2):
            where = pl.ds(side * SUMS + first, 16)
            acc[where, :] = acc[where, :] + value[:, side * PART : (side + 1) * PART]


def run_pairs(count, gathered, left, right, target_of, table, acc):
    for lane in range(BATCH):
        target_of[count + lane] = LEAF
    lax.fori_loop(0, (count + 7) // 8, lambda g, c: (source_rows(gathered, left, right, g), c)[1], 0)
    lax.fori_loop(
        0,
        (count + BATCH - 1) // BATCH,
        lambda s, c: (pair_batch(s, target_of, table, left, right, acc), c)[1],
        0,
    )


def local_kernel(ids, near, counts, pos, stren, cores, acc, table, lists,
                 own, centres, gathered, left, right, target_of, owner_of):
    own[pl.ds(0, 96), :] = jnp.concatenate([pos[k] for k in range(3)], axis=0)
    own[pl.ds(96, 96), :] = jnp.concatenate([stren[k] for k in range(3)], axis=0)
    own[pl.ds(192, 32), :] = cores[...]
    own[pl.ds(224, 32), :] = jnp.zeros((LEAF, PART), f32)
    build_targets(pos, stren, centres, table)
    acc[...] = jnp.zeros_like(acc)
    me = ids[0]
    for k in range(7):
        owner_of[ids[k + 1]] = k + 1
    owner_of[me] = 0
    for k in range(8):
        lists[PAIRS * 8 + k] = 0

    def leaf(t, place):
        used = counts[t]
        centre = centres[pl.ds(pl.multiple_of(t * 8, 8), 8), :]
        for slot in range(SLOTS):
            listed = near[t, slot]
            local = listed & (LEAF - 1)
            who = owner_of[listed >> 5]

            @pl.when((slot < used) & (who == 0))
            def _():
                gathered[pl.ds(pl.multiple_of(place * 8, 8), 8), :] = (
                    own[pl.ds(local, 8, stride=LEAF), :] - centre
                )
                target_of[place] = t

            @pl.when((slot < used) & (who > 0))
            def _():
                filled = lists[PAIRS * 8 + who]
                lists[who * PAIRS + filled] = t * LEAF + local
                lists[PAIRS * 8 + who] = filled + 1

            place = place + ((slot < used) & (who == 0)).astype(i32)
        return place

    count = lax.fori_loop(0, LEAF, leaf, 0)
    run_pairs(count, gathered, left, right, target_of, table, acc)


def remote_kernel(lists, pos, stren, far, table, acc_in, *rest):
    parts, (velocity, stretching, acc, centres, gathered, left, right, target_of) = rest[:7], rest[7:]
    acc[...] = acc_in[...]
    zero = jnp.zeros((8, PART), f32)
    for group in range(LEAF // 8):
        _, centre, _ = leaf_rows(pos, group)
        for k in range(8):
            row = jnp.broadcast_to(centre[k], (8, PART)) if k < 3 else zero
            centres[pl.ds(group * 64 + k, 8, stride=8), :] = row

    place = 0
    for k in range(7):
        count = lists[PAIRS * 8 + k + 1]

        def one(n, _, k=k, place=place):
            code = lists[(k + 1) * PAIRS + n]
            target, local = code >> 5, code & (LEAF - 1)
            centre = centres[pl.ds(pl.multiple_of(target * 8, 8), 8), :]
            gathered[pl.ds(pl.multiple_of((place + n) * 8, 8), 7), :] = (
                parts[k][pl.ds(local, 7, stride=EDGE), :] - centre[:7]
            )
            target_of[place + n] = target
            return 0

        lax.fori_loop(0, count, one, 0)
        place = place + count
    run_pairs(place, gathered, left, right, target_of, table, acc)

    coefs = far[...].T
    for group in range(LEAF // 8):
        rows = pl.ds(group * 8, 8)
        _, _, off = leaf_rows(pos, group)
        a = [stren[k, rows, :] for k in range(3)]

        def summed(row, side):
            first = side * SUMS + group * 128 + row
            high = acc[pl.ds(first, 8, stride=16), :]
            return high + acc[pl.ds(first + 6, 8, stride=16), :]

        ka = [summed(k, 0) for k in range(3)]
        kc = [summed(3 + k, 0) for k in range(3)]
        wa = [summed(k, 1) for k in range(3)]
        wc = [summed(3 + k, 1) for k in range(3)]
        coef = [coefs[group * 8 : group * 8 + 8, k : k + 1] for k in range(12)]
        for i in range(3):
            j, k = (i + 1) % 3, (i + 2) % 3
            near_vel = off[j] * ka[k] - off[k] * ka[j] - kc[i]
            steep = off[j] * wa[k] - off[k] * wa[j] - wc[i]
            near_str = a[j] * ka[k] - a[k] * ka[j] - 3.0 * steep
            grad = [coef[3 + 3 * i + m] for m in range(3)]
            velocity[i, rows, :] = (
                -inv_four_pi * near_vel + coef[i]
                + grad[0] * off[0] + grad[1] * off[1] + grad[2] * off[2]
            )
            stretching[i, rows, :] = (
                -inv_four_pi * near_str + grad[0] * a[0] + grad[1] * a[1] + grad[2] * a[2]
            )


VM = pl.BlockSpec(memory_space=pltpu.VMEM)
SM = pl.BlockSpec(memory_space=pltpu.SMEM)
PARAMS = pltpu.CompilerParams(vmem_limit_bytes=40 * 2**20)


def pair_scratch():
    return [
        pltpu.VMEM((LEAF * 8, PART), f32),
        pltpu.VMEM((ROOM * 8, PART), f32),
        pltpu.VMEM((ROOM * 24, PART), f32),
        pltpu.VMEM((ROOM * 16, PART), f32),
        pltpu.SMEM((ROOM,), i32),
    ]


def body(positions, strengths, cores, far_coef, near_list, near_count):
    bits, sects = lax.axis_size("bit"), lax.axis_size("sect")
    bit, sect = lax.axis_index("bit"), lax.axis_index("sect")
    edge = jnp.concatenate(
        [positions[:, :EDGE], strengths[:, :EDGE], cores[None, :EDGE]], axis=0
    ).reshape(7 * EDGE, PART)
    masks = [1 << n for n in range(bits.bit_length() - 1)]
    moved = [
        lax.ppermute(edge, "sect", [(i, (i + 1) % sects) for i in range(sects)]),
        lax.ppermute(edge, "sect", [((i + 1) % sects, i) for i in range(sects)]),
    ] + [lax.ppermute(edge, "bit", [(i, i ^ m) for i in range(bits)]) for m in masks]
    own = bit * sects + sect
    ids = jnp.stack(
        [own, bit * sects + (sect - 1) % sects, bit * sects + (sect + 1) % sects]
        + [(bit ^ m) * sects + sect for m in masks]
    ).astype(i32)
    acc, table, lists = pl.pallas_call(
        local_kernel,
        out_shape=(
            jax.ShapeDtypeStruct((2 * SUMS, PART), f32),
            jax.ShapeDtypeStruct((2 * TABLE, PART), f32),
            jax.ShapeDtypeStruct((PAIRS * 8 + 8,), i32),
        ),
        in_specs=[SM, SM, SM, VM, VM, VM],
        out_specs=(VM, VM, SM),
        scratch_shapes=[pltpu.VMEM((LEAF * 8, PART), f32)] + pair_scratch()
        + [pltpu.SMEM((bits * sects,), i32)],
        compiler_params=PARAMS,
        name="local_pairs",
    )(ids, near_list, near_count, positions, strengths, cores)
    return pl.pallas_call(
        remote_kernel,
        out_shape=(
            jax.ShapeDtypeStruct((3, LEAF, PART), f32),
            jax.ShapeDtypeStruct((3, LEAF, PART), f32),
        ),
        in_specs=[SM] + [VM] * 12,
        out_specs=(VM, VM),
        scratch_shapes=[pltpu.VMEM((2 * SUMS, PART), f32)] + pair_scratch(),
        compiler_params=PARAMS,
        name="remote_pairs",
    )(lists, positions, strengths, far_coef, table, acc, *moved)


def solution(mesh):
    in_specs = (
        P(None, ("bit", "sect"), None),
        P(None, ("bit", "sect"), None),
        P(("bit", "sect"), None),
        P(None, ("bit", "sect")),
        P(("bit", "sect"), None),
        P(("bit", "sect")),
    )
    out_specs = (P(None, ("bit", "sect"), None), P(None, ("bit", "sect"), None))
    return jax.shard_map(body, mesh=mesh, in_specs=in_specs, out_specs=out_specs, check_vma=False)
```

```python
import math

import jax
import jax.numpy as jnp
from jax import lax
from jax.experimental import pallas as pl
from jax.experimental.pallas import tpu as pltpu
from jax.sharding import PartitionSpec as P

inv_four_pi = 1.0 / (4.0 * math.pi)
f32, bf16, i32 = jnp.float32, jnp.bfloat16, jnp.int32

LEAF = 32
PART = 128
SLOTS = 8
EDGE = 24
FIELDS = 7
MOVED = FIELDS * EDGE
PAIRS = LEAF * SLOTS
BATCH = 16
ROOM = PAIRS + BATCH
TABLE = (LEAF + 1) * 32
SUMS = (LEAF + 1) * 16
N_LOCAL, N_REMOTE, N_DONE = 2 * ROOM, 2 * ROOM + 1, 2 * ROOM + 2
NOTES = 2 * ROOM + 8


def rounded(value):
    return value.astype(bf16).astype(f32)


def split3(value):
    high = rounded(value)
    rest = value - high
    mid = rounded(rest)
    return high, mid, rest - mid


def split2(value):
    high = value.astype(bf16)
    return high, (value - high.astype(f32)).astype(bf16)


def leaf_fields(own, group, fields):
    return [own[pl.ds(k * LEAF + group * 8, 8), :] for k in fields]


def offsets(own, group):
    point = leaf_fields(own, group, range(3))
    centre = [jnp.mean(v, axis=1, keepdims=True) for v in point]
    return centre, [v - c for v, c in zip(point, centre)]


def build_targets(own, centres, table, stage):
    for group in range(LEAF // 8):
        centre, off = offsets(own, group)
        a = leaf_fields(own, group, range(3, 6))
        zero = jnp.zeros((8, PART), f32)
        one = jnp.ones((8, PART), f32)
        for k in range(8):
            row = jnp.broadcast_to(centre[k], (8, PART)) if k < 3 else zero
            centres[pl.ds(group * 64 + k, 8, stride=8), :] = row
        left = [split3(-2.0 * v) for v in off]
        right = [split3(-v) for v in a]
        square = split3(off[0] * off[0] + off[1] * off[1] + off[2] * off[2])
        along = split3(off[0] * a[0] + off[1] * a[1] + off[2] * a[2])
        rows = []
        for part in (0, 1, 2, 0, 1, 0):
            rows += [(left[k][part], right[k][part]) for k in range(3)]
        rows += [(one, zero)] * 3
        rows += [(square[k], along[k]) for k in range(3)]
        rows += [(zero, zero)] * 8
        for k, (spread_row, proj_row) in enumerate(rows):
            stage[pl.ds(group * 512 + k, 8, stride=32), :] = spread_row
            stage[pl.ds(group * 512 + 256 + k, 8, stride=32), :] = proj_row
        for side in range(2):
            table[pl.ds(side * TABLE + group * 256, 256), :] = stage[
                pl.ds(group * 512 + side * 256, 256), :
            ].astype(bf16)


def source_rows(gathered, left, right, stage, group):
    first = pl.multiple_of(group * 64, 64)
    q = [gathered[pl.ds(first + k, 8, stride=8), :] for k in range(FIELDS)]
    x, a, core = q[:3], q[3:6], q[6]
    part = [split3(v) for v in x]
    size = split3(x[0] * x[0] + x[1] * x[1] + x[2] * x[2] + core * core)
    one = jnp.ones((8, PART), f32)
    rows = []
    for level in (0, 0, 0, 1, 1, 2):
        rows += [part[k][level] for k in range(3)]
    rows += list(size) + [one] * 3 + [jnp.zeros((8, PART), f32)] * 8
    for k, row in enumerate(rows):
        stage[pl.ds(k, 8, stride=32), :] = row
    crossed = [
        x[1] * a[2] - x[2] * a[1],
        x[2] * a[0] - x[0] * a[2],
        x[0] * a[1] - x[1] * a[0],
    ]
    for k, row in enumerate(a + crossed):
        high = rounded(row)
        stage[pl.ds(256 + k, 8, stride=16), :] = high
        stage[pl.ds(262 + k, 8, stride=16), :] = row - high
    for k in range(12, 16):
        stage[pl.ds(256 + k, 8, stride=16), :] = jnp.zeros((8, PART), f32)
    left[pl.ds(pl.multiple_of(group * 256, 256), 256), :] = stage[pl.ds(0, 256), :].astype(bf16)
    right[pl.ds(pl.multiple_of(group * 128, 128), 128), :] = stage[pl.ds(256, 128), :].astype(bf16)


def pair_batch(step, target_of, table, left, right, acc, carry):
    last, total = carry
    results = []
    for lane in range(BATCH):
        pair = step * BATCH + lane
        target = target_of[pair]
        lhs = left[pl.ds(pl.multiple_of(pair * 32, 32), 32), :]
        first = pl.multiple_of(target * 32, 32)
        rhs = jnp.concatenate(
            [table[pl.ds(first, 32), :], table[pl.ds(TABLE + first, 32), :]], axis=1
        )
        both = lax.dot_general(lhs, rhs, (((0,), (0,)), ((), ())), preferred_element_type=f32)
        spread, proj = both[:, :PART], both[:, PART:]
        root = lax.rsqrt(spread)
        square = root * root
        kernel = root * square
        weight = kernel * square * proj
        k_high, k_low = split2(kernel)
        w_high, w_low = split2(weight)
        pairs = jnp.concatenate(
            [jnp.concatenate([k_high, w_high], axis=1), jnp.concatenate([k_low, w_low], axis=1)], axis=0
        )
        rows = right[pl.ds(pl.multiple_of(pair * 16, 16), 16), :]
        rows = jnp.concatenate([rows, rows], axis=1)
        results.append((target, jnp.dot(rows, pairs, preferred_element_type=f32)))
    for target, value in results:
        total = jnp.where(target == last, total, 0.0) + value
        last = target
        first = pl.multiple_of(target * 16, 16)
        for side in range(2):
            acc[pl.ds(side * SUMS + first, 16), :] = total[:, side * PART : (side + 1) * PART]
    return last, total


def features(count, gathered, left, right, stage):
    lax.fori_loop(0, (count + 7) // 8, lambda g, c: (source_rows(gathered, left, right, stage, g), c)[1], 0)


def sum_pairs(begin, end, target_of, table, left, right, acc, carry):
    lax.fori_loop(
        begin, end, lambda s, c: pair_batch(s, target_of, table, left, right, acc, c), carry
    )


def start_carry():
    return jnp.int32(-1), jnp.zeros((16, 2 * PART), f32)


def batches(count):
    return (count + BATCH - 1) // BATCH


def early_batches(me):
    z, y = (me >> 3) & 7, me >> 6
    return jnp.where(z == 0, jnp.where(y < 2, 4, 3), jnp.where(z == 1, 2, 0)).astype(i32)


def scan(codes, own, centres, gathered, notes):
    row = lax.broadcasted_iota(i32, (8, PART), 0)
    stren = (row >= 3) & (row < 6)

    def leaf(t, carry):
        place, outside = carry
        centre = centres[pl.ds(pl.multiple_of(t * 8, 8), 8), :]
        for slot in range(SLOTS):
            code = codes[slot, t]
            times = ((code >> 2) & 15).astype(f32)
            source = own[pl.ds((code >> 6) & (LEAF - 1), 8, stride=LEAF), :] - centre
            gathered[pl.ds(pl.multiple_of(place * 8, 8), 8), :] = jnp.where(stren, source * times, source)
            notes[place] = t
            notes[ROOM + outside] = (t << 20) | code
            place = place + (code & 1)
            outside = outside + ((code >> 1) & 1)
        return place, outside

    place, outside = lax.fori_loop(0, LEAF, leaf, (jnp.int32(0), jnp.int32(0)))
    for lane in range(BATCH):
        notes[place + lane] = LEAF
    notes[N_LOCAL] = place
    notes[N_REMOTE] = outside


def prepare(codes, own, centres, table, gathered, left, right, acc, notes, stage):
    build_targets(own, centres, table, stage)
    acc[...] = jnp.zeros_like(acc)
    scan(codes, own, centres, gathered, notes)
    features(notes[N_LOCAL], gathered, left, right, stage)


def slot_codes(near, counts):
    slot = lax.broadcasted_iota(i32, near.shape, 0)
    used = slot < counts
    times = jnp.ones(near.shape, i32)
    fresh = used
    for d in range(1, SLOTS):
        after = pltpu.roll(near, SLOTS - d, 0)
        times = times + ((after == near) & (slot + d < counts)).astype(i32)
        before = pltpu.roll(near, d, 0)
        fresh = fresh & ~((before == near) & (slot >= d))
    leaf = near & (LEAF - 1)
    owner = near >> 5
    me = jnp.broadcast_to(near[0:1, 0:1] >> 5, near.shape)
    differs = owner ^ me
    bit = differs >> 3
    part = jnp.where(bit == 0, jnp.where(differs == 1, 0, 1), 2)
    for n in range(1, 5):
        part = jnp.where(bit == 1 << n, 2 + n, part)
    mine = differs == 0
    row = jnp.where(mine, leaf, part * MOVED + leaf)
    code = jnp.where(mine, 1, 2) + times * 4 + row * 64
    return jnp.where(fresh, code, 0)


def front_kernel(pos, stren, cores, near, counts, own, edge, codes, notes, centres, table, left, right, acc,
                 gathered, stage, near_v, counts_v, codes_s, sems):
    copies = []
    for k in range(FIELDS):
        ref, base = ((pos, k), (stren, k - 3), (cores, 0))[min(k // 3, 2)]
        copies.append((ref.at[pl.ds(base * LEAF, EDGE)], edge.at[pl.ds(k * EDGE, EDGE)]))
    copies += [
        (pos, own.at[pl.ds(0, 96)]),
        (stren, own.at[pl.ds(96, 96)]),
        (cores, own.at[pl.ds(192, 32)]),
        (near, near_v),
        (counts, counts_v),
    ]
    copies = [pltpu.make_async_copy(a, b, sems.at[n]) for n, (a, b) in enumerate(copies)]
    for copy in copies:
        copy.start()
    own[pl.ds(224, 32), :] = jnp.zeros((LEAF, PART), f32)
    for copy in copies:
        copy.wait()
    codes[...] = slot_codes(near_v[...], counts_v[...])
    fetch = pltpu.make_async_copy(codes, codes_s, sems.at[0])
    fetch.start()
    fetch.wait()
    limit = early_batches(lax.axis_index("bit") * 8 + lax.axis_index("sect"))
    notes[N_DONE] = 0

    @pl.when(limit > 0)
    def _():
        prepare(codes_s, own, centres, table, gathered, left, right, acc, notes, stage)
        done = jnp.minimum(batches(notes[N_LOCAL]), limit)
        sum_pairs(0, done, notes, table, left, right, acc, start_carry())
        notes[N_DONE] = done


def local_kernel(notes_in, codes, own, centres0, table0, left0, right0, acc0,
                 notes, centres, table, acc, gathered, left, right, stage):
    done = notes_in[N_DONE]

    @pl.when(done == 0)
    def _():
        prepare(codes, own, centres, table, gathered, left, right, acc, notes, stage)
        sum_pairs(0, batches(notes[N_LOCAL]), notes, table, left, right, acc, start_carry())

    @pl.when(done > 0)
    def _():
        centres[...] = centres0[...]
        table[...] = table0[...]
        acc[...] = acc0[...]

    @pl.when((done > 0) & (done < batches(notes_in[N_LOCAL])))
    def _():
        last = notes_in[done * BATCH - 1]
        first = pl.multiple_of(last * 16, 16)
        total = jnp.concatenate([acc[pl.ds(side * SUMS + first, 16), :] for side in range(2)], axis=1)
        sum_pairs(done, batches(notes_in[N_LOCAL]), notes_in, table0, left0, right0, acc, (last, total))


def remote_kernel(notes0, notes1, own, centres, table, acc, far, *rest):
    parts, (velocity, stretching, pool, far_v, gathered, left, right, stage, outer, targets, sems) = rest[:7], rest[7:]
    copies = [
        pltpu.make_async_copy(ref, pool.at[pl.ds(k * MOVED, MOVED)], sems.at[k]) for k, ref in enumerate(parts)
    ] + [pltpu.make_async_copy(far, far_v, sems.at[7])]
    for copy in copies:
        copy.start()
    outer[...] = jnp.zeros_like(outer)
    early = notes0[N_DONE] > 0
    row = lax.broadcasted_iota(i32, (FIELDS, PART), 0)
    stren = (row >= 3) & (row < 6)
    for copy in copies:
        copy.wait()

    def gather(notes):
        def one(n, _):
            code = notes[ROOM + n]
            target = code >> 20
            times = ((code >> 2) & 15).astype(f32)
            centre = centres[pl.ds(pl.multiple_of(target * 8, 8), 8), :][:FIELDS]
            source = pool[pl.ds((code >> 6) & 2047, FIELDS, stride=EDGE), :] - centre
            gathered[pl.ds(pl.multiple_of(n * 8, 8), FIELDS), :] = jnp.where(stren, source * times, source)
            targets[n] = target
            return 0

        lax.fori_loop(0, notes[N_REMOTE], one, 0)
        for lane in range(BATCH):
            targets[notes[N_REMOTE] + lane] = LEAF

    pl.when(early)(lambda: gather(notes0))
    pl.when(jnp.logical_not(early))(lambda: gather(notes1))
    count = jnp.where(early, notes0[N_REMOTE], notes1[N_REMOTE])
    features(count, gathered, left, right, stage)
    sum_pairs(0, batches(count), targets, table, left, right, outer, start_carry())

    coefs = far_v[...].T
    for group in range(LEAF // 8):
        rows = pl.ds(group * 8, 8)
        _, off = offsets(own, group)
        a = leaf_fields(own, group, range(3, 6))

        def summed(field, side):
            first = side * SUMS + group * 128 + field
            parts = [
                ref[pl.ds(first + low, 8, stride=16), :] for ref in (acc, outer) for low in (0, 6)
            ]
            return (parts[0] + parts[1]) + (parts[2] + parts[3])

        ka = [summed(k, 0) for k in range(3)]
        kc = [summed(3 + k, 0) for k in range(3)]
        wa = [summed(k, 1) for k in range(3)]
        wc = [summed(3 + k, 1) for k in range(3)]
        coef = [coefs[group * 8 : group * 8 + 8, k : k + 1] for k in range(12)]
        for i in range(3):
            j, k = (i + 1) % 3, (i + 2) % 3
            near_vel = off[j] * ka[k] - off[k] * ka[j] - kc[i]
            steep = off[j] * wa[k] - off[k] * wa[j] - wc[i]
            near_str = a[j] * ka[k] - a[k] * ka[j] - 3.0 * steep
            grad = [coef[3 + 3 * i + m] for m in range(3)]
            velocity[i, rows, :] = (
                -inv_four_pi * near_vel + coef[i]
                + grad[0] * off[0] + grad[1] * off[1] + grad[2] * off[2]
            )
            stretching[i, rows, :] = (
                -inv_four_pi * near_str + grad[0] * a[0] + grad[1] * a[1] + grad[2] * a[2]
            )


VM = pl.BlockSpec(memory_space=pltpu.VMEM)
SM = pl.BlockSpec(memory_space=pltpu.SMEM)
HB = pl.BlockSpec(memory_space=pltpu.HBM)
PARAMS = pltpu.CompilerParams(vmem_limit_bytes=24 * 2**20)


def body(positions, strengths, cores, far_coef, near_list, near_count):
    bits, sects = lax.axis_size("bit"), lax.axis_size("sect")
    shape = jax.ShapeDtypeStruct
    work = [
        shape((NOTES,), i32),
        shape((LEAF * 8, PART), f32),
        shape((2 * TABLE, PART), bf16),
        shape((ROOM * 32, PART), bf16),
        shape((ROOM * 16, PART), bf16),
        shape((2 * SUMS, PART), f32),
    ]
    gather_room = pltpu.VMEM((ROOM * 8, PART), f32)
    source_room = [
        pltpu.VMEM((ROOM * 32, PART), bf16),
        pltpu.VMEM((ROOM * 16, PART), bf16),
        pltpu.VMEM((2048, PART), f32),
    ]
    fixed = [
        pltpu.with_memory_space_constraint(v, pltpu.HBM)
        for v in (
            positions.reshape(3 * LEAF, PART),
            strengths.reshape(3 * LEAF, PART),
            cores,
            near_list.T,
            near_count.reshape(1, LEAF),
            far_coef,
        )
    ]
    own, edge, codes, notes0, *held = pl.pallas_call(
        front_kernel,
        out_shape=[
            shape((LEAF * 8, PART), f32),
            shape((MOVED, PART), f32),
            shape((SLOTS, LEAF), i32),
        ] + work,
        in_specs=[HB] * 5,
        out_specs=[VM, VM, VM, SM] + [VM] * 5,
        scratch_shapes=[
            gather_room,
            source_room[2],
            pltpu.VMEM((SLOTS, LEAF), i32),
            pltpu.VMEM((1, LEAF), i32),
            pltpu.SMEM((SLOTS, LEAF), i32),
            pltpu.SemaphoreType.DMA((12,)),
        ],
        compiler_params=PARAMS,
        name="front",
    )(*fixed[:5])
    moved = [lax.ppermute(edge, "bit", [(i, i ^ (1 << n)) for i in range(bits)]) for n in (0, 3, 4, 1, 2)]
    beside = [(i, i + 1) for i in range(1, sects - 1, 2)] + [(sects - 1, 0)]
    moved.append(lax.ppermute(edge, "sect", beside + [(j, i) for i, j in beside]))
    moved.append(lax.ppermute(edge, "sect", [(i, i ^ 1) for i in range(sects)]))
    z1, y1, y2, z2, z4, outer, inner = moved
    notes1, centres, table, acc = pl.pallas_call(
        local_kernel,
        out_shape=[work[n] for n in (0, 1, 2, 5)],
        in_specs=[SM, SM] + [VM] * 6,
        out_specs=[SM] + [VM] * 3,
        scratch_shapes=[gather_room] + source_room,
        compiler_params=PARAMS,
        name="local_pairs",
    )(notes0, codes, own, *held)
    return pl.pallas_call(
        remote_kernel,
        out_shape=[shape((3, LEAF, PART), f32)] * 2,
        in_specs=[SM, SM] + [VM] * 4 + [HB] + [VM] * 7,
        out_specs=[VM, VM],
        scratch_shapes=[
            pltpu.VMEM((7 * MOVED, PART), f32),
            pltpu.VMEM((12, LEAF), f32),
            gather_room,
            *source_room,
            pltpu.VMEM((2 * SUMS, PART), f32),
            pltpu.SMEM((ROOM,), i32),
            pltpu.SemaphoreType.DMA((8,)),
        ],
        compiler_params=PARAMS,
        name="remote_pairs",
    )(notes0, notes1, own, centres, table, acc, fixed[5], inner, outer, z1, z2, z4, y1, y2)


def solution(mesh):
    in_specs = (
        P(None, ("bit", "sect"), None),
        P(None, ("bit", "sect"), None),
        P(("bit", "sect"), None),
        P(None, ("bit", "sect")),
        P(("bit", "sect"), None),
        P(("bit", "sect")),
    )
    out_specs = (P(None, ("bit", "sect"), None), P(None, ("bit", "sect"), None))
    return jax.shard_map(body, mesh=mesh, in_specs=in_specs, out_specs=out_specs, check_vma=False)
```

```python
import math

import jax
import jax.numpy as jnp
from jax import lax
from jax.experimental import pallas as pl
from jax.experimental.pallas import tpu as pltpu
from jax.sharding import PartitionSpec as P

inv_four_pi = 1.0 / (4.0 * math.pi)
f32, bf16, i32 = jnp.float32, jnp.bfloat16, jnp.int32

LEAF = 32
PART = 128
SLOTS = 8
EDGE = 24
FIELDS = 7
MOVED = FIELDS * EDGE
PAIRS = LEAF * SLOTS
BATCH = 16
HALF = BATCH // 2
ROOM = PAIRS + 2 * BATCH
TABLE = (LEAF + 1) * 32
SUMS = (LEAF + 1) * 16
N_LOCAL, N_REMOTE, N_DONE = 2 * ROOM, 2 * ROOM + 1, 2 * ROOM + 2
NOTES = 2 * ROOM + 8


def rounded(value):
    return value.astype(bf16).astype(f32)


def split3(value):
    high = rounded(value)
    rest = value - high
    mid = rounded(rest)
    return high, mid, rest - mid


def split2(value):
    high = value.astype(bf16)
    return high, (value - high.astype(f32)).astype(bf16)


def leaf_fields(own, group, fields):
    return [own[pl.ds(k * LEAF + group * 8, 8), :] for k in fields]


def offsets(own, group):
    point = leaf_fields(own, group, range(3))
    centre = [jnp.mean(v, axis=1, keepdims=True) for v in point]
    return centre, [v - c for v, c in zip(point, centre)]


def build_targets(own, centres, table, stage):
    for group in range(LEAF // 8):
        centre, off = offsets(own, group)
        a = leaf_fields(own, group, range(3, 6))
        zero = jnp.zeros((8, PART), f32)
        one = jnp.ones((8, PART), f32)
        for k in range(8):
            row = jnp.broadcast_to(centre[k], (8, PART)) if k < 3 else zero
            centres[pl.ds(group * 64 + k, 8, stride=8), :] = row
        left = [split3(-2.0 * v) for v in off]
        right = [split3(-v) for v in a]
        square = split3(off[0] * off[0] + off[1] * off[1] + off[2] * off[2])
        along = split3(off[0] * a[0] + off[1] * a[1] + off[2] * a[2])
        rows = []
        for part in (0, 1, 2, 0, 1, 0):
            rows += [(left[k][part], right[k][part]) for k in range(3)]
        rows += [(one, zero)] * 3
        rows += [(square[k], along[k]) for k in range(3)]
        rows += [(zero, zero)] * 8
        for k, (spread_row, proj_row) in enumerate(rows):
            stage[pl.ds(group * 512 + k, 8, stride=32), :] = spread_row
            stage[pl.ds(group * 512 + 256 + k, 8, stride=32), :] = proj_row
        for side in range(2):
            table[pl.ds(side * TABLE + group * 256, 256), :] = stage[
                pl.ds(group * 512 + side * 256, 256), :
            ].astype(bf16)


def source_rows(gathered, left, right, group):
    first = pl.multiple_of(group * 64, 64)
    q = [gathered[pl.ds(first + k, 8, stride=8), :] for k in range(FIELDS)]
    x, a, core = q[:3], q[3:6], q[6]
    part = [split3(v) for v in x]
    size = split3(x[0] * x[0] + x[1] * x[1] + x[2] * x[2] + core * core)
    one = jnp.ones((8, PART), f32)
    rows = []
    for level in (0, 0, 0, 1, 1, 2):
        rows += [part[k][level] for k in range(3)]
    rows += list(size) + [one] * 3
    base = pl.multiple_of(group * 192, 64)
    for k, row in enumerate(rows):
        left[pl.ds(base + k, 8, stride=24), :] = row
    crossed = [
        x[1] * a[2] - x[2] * a[1],
        x[2] * a[0] - x[0] * a[2],
        x[0] * a[1] - x[1] * a[0],
    ]
    base = pl.multiple_of(group * 128, 128)
    for k, row in enumerate(a + crossed):
        high = rounded(row)
        right[pl.ds(base + k, 8, stride=16), :] = high
        right[pl.ds(base + 6 + k, 8, stride=16), :] = row - high
    for k in range(12, 16):
        right[pl.ds(base + k, 8, stride=16), :] = jnp.zeros((8, PART), f32)


def pair_products(pair, target, table, left):
    lhs = left[pl.ds(pl.multiple_of(pair * 24, 8), 24), :]
    lhs = jnp.concatenate([lhs, jnp.zeros((8, PART), f32)], axis=0).astype(bf16)
    first = pl.multiple_of(target * 32, 32)
    rhs = jnp.concatenate([table[pl.ds(first, 32), :], table[pl.ds(TABLE + first, 32), :]], axis=1)
    return lax.dot_general(lhs, rhs, (((0,), (0,)), ((), ())), preferred_element_type=f32)


def pair_total(pair, both, right):
    spread, proj = both[:, :PART], both[:, PART:]
    root = lax.rsqrt(spread)
    square = root * root
    kernel = root * square
    weight = kernel * square * proj
    k_high, k_low = split2(kernel)
    w_high, w_low = split2(weight)
    pairs = jnp.concatenate(
        [jnp.concatenate([k_high, w_high], axis=1), jnp.concatenate([k_low, w_low], axis=1)], axis=0
    )
    rows = right[pl.ds(pl.multiple_of(pair * 16, 16), 16), :].astype(bf16)
    rows = jnp.concatenate([rows, rows], axis=1)
    return jnp.dot(rows, pairs, preferred_element_type=f32)


def half_batch(begin, now, later, target_of, table, left, right, acc, carry):
    last, total = carry
    results = []
    for lane in range(HALF):
        pair = begin + lane
        ahead = pair + HALF
        later[lane] = pair_products(ahead, target_of[ahead], table, left)
        results.append((target_of[pair], pair_total(pair, now[lane], right)))
    for target, value in results:
        total = jnp.where(target == last, total, 0.0) + value
        last = target
        first = pl.multiple_of(target * 16, 16)
        for side in range(2):
            acc[pl.ds(side * SUMS + first, 16), :] = total[:, side * PART : (side + 1) * PART]
    return last, total


def features(count, gathered, left, right):
    lax.fori_loop(0, (count + 7) // 8, lambda g, c: (source_rows(gathered, left, right, g), c)[1], 0)


def sum_pairs(begin, end, target_of, table, left, right, acc, products, carry):
    even, odd = products
    work = (target_of, table, left, right, acc)

    @pl.when(begin < end)
    def _():
        for lane in range(HALF):
            pair = begin * BATCH + lane
            even[lane] = pair_products(pair, target_of[pair], table, left)

    def step(s, c):
        c = half_batch(s * BATCH, even, odd, *work, c)
        return half_batch(s * BATCH + HALF, odd, even, *work, c)

    lax.fori_loop(begin, end, step, carry)


def start_carry():
    return jnp.int32(-1), jnp.zeros((16, 2 * PART), f32)


def batches(count):
    return (count + BATCH - 1) // BATCH


def early_batches(me, count):
    z = (me >> 3) & 7
    later = jnp.where(z < 2, 4, 99)
    return jnp.minimum(jnp.maximum(batches(count) - later, 0), 5)


def scan(codes, own, centres, gathered, notes):
    row = lax.broadcasted_iota(i32, (8, PART), 0)
    stren = (row >= 3) & (row < 6)

    def leaf(t, carry):
        place, outside = carry
        centre = centres[pl.ds(pl.multiple_of(t * 8, 8), 8), :]
        for slot in range(SLOTS):
            code = codes[slot, t]
            times = ((code >> 2) & 15).astype(f32)
            source = own[pl.ds((code >> 6) & (LEAF - 1), 8, stride=LEAF), :] - centre
            gathered[pl.ds(pl.multiple_of(place * 8, 8), 8), :] = jnp.where(stren, source * times, source)
            notes[place] = t
            notes[ROOM + outside] = (t << 20) | code
            place = place + (code & 1)
            outside = outside + ((code >> 1) & 1)
        return place, outside

    place, outside = lax.fori_loop(0, LEAF, leaf, (jnp.int32(0), jnp.int32(0)))
    for lane in range(2 * BATCH):
        notes[place + lane] = LEAF
    notes[N_LOCAL] = place
    notes[N_REMOTE] = outside


def prepare(own, centres, table, gathered, left, right, acc, notes, stage, codes, codes_s, sem):
    fetch = pltpu.make_async_copy(codes, codes_s, sem.at[0])
    fetch.start()
    build_targets(own, centres, table, stage)
    acc[...] = jnp.zeros_like(acc)
    fetch.wait()
    scan(codes_s, own, centres, gathered, notes)
    features(notes[N_LOCAL], gathered, left, right)


def slot_codes(near, counts):
    slot = lax.broadcasted_iota(i32, near.shape, 0)
    used = slot < counts
    times = jnp.ones(near.shape, i32)
    fresh = used
    for d in range(1, SLOTS):
        after = pltpu.roll(near, SLOTS - d, 0)
        times = times + ((after == near) & (slot + d < counts)).astype(i32)
        before = pltpu.roll(near, d, 0)
        fresh = fresh & ~((before == near) & (slot >= d))
    leaf = near & (LEAF - 1)
    owner = near >> 5
    me = jnp.broadcast_to(near[0:1, 0:1] >> 5, near.shape)
    differs = owner ^ me
    bit = differs >> 3
    part = jnp.where(bit == 0, jnp.where(differs == 1, 0, 1), 2)
    for n in range(1, 5):
        part = jnp.where(bit == 1 << n, 2 + n, part)
    mine = differs == 0
    row = jnp.where(mine, leaf, part * LEAF + leaf)
    code = jnp.where(mine, 1, 2) + times * 4 + row * 64
    return jnp.where(fresh, code, 0)


def front_kernel(pos, stren, cores, near, counts, own, edge, near_v, counts_v, notes, centres, table,
                 left, right, acc, gathered, sems, even, odd, stage, codes, codes_s, sem):
    copies = []
    for k in range(FIELDS):
        ref, base = ((pos, k), (stren, k - 3), (cores, 0))[min(k // 3, 2)]
        copies.append((ref.at[pl.ds(base * LEAF, EDGE)], edge.at[pl.ds(k * EDGE, EDGE)]))
    copies += [
        (pos, own.at[pl.ds(0, 96)]),
        (stren, own.at[pl.ds(96, 96)]),
        (cores, own.at[pl.ds(192, 32)]),
        (near, near_v),
        (counts, counts_v),
    ]
    copies = [pltpu.make_async_copy(a, b, sems.at[n]) for n, (a, b) in enumerate(copies)]
    for copy in copies:
        copy.start()
    own[pl.ds(224, 32), :] = jnp.zeros((LEAF, PART), f32)
    me = lax.axis_index("bit") * lax.axis_size("sect") + lax.axis_index("sect")
    notes[N_DONE] = 0
    for copy in copies:
        copy.wait()

    @pl.when(me & 32 == 0)
    def _():
        found = slot_codes(near_v[...], counts_v[...])
        codes[...] = found
        done = early_batches(me, jnp.sum((found & 1).astype(f32)).astype(i32))

        @pl.when(done > 0)
        def _():
            prepare(own, centres, table, gathered, left, right, acc, notes, stage, codes, codes_s, sem)
            sum_pairs(0, done, notes, table, left, right, acc, (even, odd), start_carry())
            notes[N_DONE] = done


def local_kernel(notes_in, near, counts, own, centres0, table0, left0, right0, acc0,
                 notes, centres, table, acc, gathered, left, right, even, odd, stage, codes, codes_s, sem):
    done = notes_in[N_DONE]

    @pl.when(done == 0)
    def _():
        codes[...] = slot_codes(near[...], counts[...])
        prepare(own, centres, table, gathered, left, right, acc, notes, stage, codes, codes_s, sem)
        sum_pairs(0, batches(notes[N_LOCAL]), notes, table, left, right, acc, (even, odd), start_carry())

    @pl.when(done > 0)
    def _():
        centres[...] = centres0[...]
        table[...] = table0[...]
        acc[...] = acc0[...]

    @pl.when((done > 0) & (done < batches(notes_in[N_LOCAL])))
    def _():
        last = notes_in[done * BATCH - 1]
        first = pl.multiple_of(last * 16, 16)
        total = jnp.concatenate([acc[pl.ds(side * SUMS + first, 16), :] for side in range(2)], axis=1)
        carry = (last, total)
        sum_pairs(done, batches(notes_in[N_LOCAL]), notes_in, table0, left0, right0, acc, (even, odd), carry)


def remote_kernel(notes0, notes1, own, centres, table, acc, far, *rest):
    p1, p8, p16, p2, p4, outer_part, inner_part = rest[:7]
    parts = (inner_part, outer_part, p1, p2, p4, p8, p16)
    (velocity, stretching, far_v, gathered, left, right, even, odd, outer, targets, sems) = rest[7:]
    copy = pltpu.make_async_copy(far, far_v, sems.at[0])
    copy.start()
    outer[...] = jnp.zeros_like(outer)
    early = notes0[N_DONE] > 0
    row = lax.broadcasted_iota(i32, (FIELDS, PART), 0)
    stren = (row >= 3) & (row < 6)

    def gather(notes):
        def one(n, _):
            code = notes[ROOM + n]
            target = code >> 20
            times = ((code >> 2) & 15).astype(f32)
            where = pl.ds((code >> 6) & (LEAF - 1), FIELDS, stride=EDGE)
            part = (code >> 11) & 7
            source = parts[0][where, :]
            for k in range(1, 7):
                source = jnp.where(part == k, parts[k][where, :], source)
            source = source - centres[pl.ds(pl.multiple_of(target * 8, 8), 8), :][:FIELDS]
            gathered[pl.ds(pl.multiple_of(n * 8, 8), FIELDS), :] = jnp.where(stren, source * times, source)
            targets[n] = target
            return 0

        lax.fori_loop(0, notes[N_REMOTE], one, 0)
        for lane in range(2 * BATCH):
            targets[notes[N_REMOTE] + lane] = LEAF

    pl.when(early)(lambda: gather(notes0))
    pl.when(jnp.logical_not(early))(lambda: gather(notes1))
    count = jnp.where(early, notes0[N_REMOTE], notes1[N_REMOTE])
    features(count, gathered, left, right)
    sum_pairs(0, batches(count), targets, table, left, right, outer, (even, odd), start_carry())

    copy.wait()
    coefs = far_v[...].T
    for group in range(LEAF // 8):
        rows = pl.ds(group * 8, 8)
        _, off = offsets(own, group)
        a = leaf_fields(own, group, range(3, 6))

        def summed(field, side):
            first = side * SUMS + group * 128 + field
            parts = [
                ref[pl.ds(first + low, 8, stride=16), :] for ref in (acc, outer) for low in (0, 6)
            ]
            return (parts[0] + parts[1]) + (parts[2] + parts[3])

        ka = [summed(k, 0) for k in range(3)]
        kc = [summed(3 + k, 0) for k in range(3)]
        wa = [summed(k, 1) for k in range(3)]
        wc = [summed(3 + k, 1) for k in range(3)]
        coef = [coefs[group * 8 : group * 8 + 8, k : k + 1] for k in range(12)]
        for i in range(3):
            j, k = (i + 1) % 3, (i + 2) % 3
            near_vel = off[j] * ka[k] - off[k] * ka[j] - kc[i]
            steep = off[j] * wa[k] - off[k] * wa[j] - wc[i]
            near_str = a[j] * ka[k] - a[k] * ka[j] - 3.0 * steep
            grad = [coef[3 + 3 * i + m] for m in range(3)]
            velocity[i, rows, :] = (
                -inv_four_pi * near_vel + coef[i]
                + grad[0] * off[0] + grad[1] * off[1] + grad[2] * off[2]
            )
            stretching[i, rows, :] = (
                -inv_four_pi * near_str + grad[0] * a[0] + grad[1] * a[1] + grad[2] * a[2]
            )


VM = pl.BlockSpec(memory_space=pltpu.VMEM)
SM = pl.BlockSpec(memory_space=pltpu.SMEM)
HB = pl.BlockSpec(memory_space=pltpu.HBM)
PARAMS = pltpu.CompilerParams(vmem_limit_bytes=24 * 2**20)


def body(positions, strengths, cores, far_coef, near_list, near_count):
    bits, sects = lax.axis_size("bit"), lax.axis_size("sect")
    shape = jax.ShapeDtypeStruct
    work = [
        shape((NOTES,), i32),
        shape((LEAF * 8, PART), f32),
        shape((2 * TABLE, PART), bf16),
        shape((ROOM * 24, PART), f32),
        shape((ROOM * 16, PART), f32),
        shape((2 * SUMS, PART), f32),
    ]
    gather_room = pltpu.VMEM((ROOM * 8, PART), f32)
    source_room = [pltpu.VMEM((ROOM * 24, PART), f32), pltpu.VMEM((ROOM * 16, PART), f32)]
    product_room = [pltpu.VMEM((HALF, PART, 2 * PART), f32)] * 2
    list_room = [
        pltpu.VMEM((2048, PART), f32),
        pltpu.VMEM((SLOTS, LEAF), i32),
        pltpu.SMEM((SLOTS, LEAF), i32),
        pltpu.SemaphoreType.DMA((1,)),
    ]
    fixed = [
        pltpu.with_memory_space_constraint(v, pltpu.HBM)
        for v in (
            positions.reshape(3 * LEAF, PART),
            strengths.reshape(3 * LEAF, PART),
            cores,
            near_list.T,
            near_count.reshape(1, LEAF),
            far_coef,
        )
    ]
    own, edge, near, counts, notes0, *held = pl.pallas_call(
        front_kernel,
        out_shape=[
            shape((LEAF * 8, PART), f32),
            shape((MOVED, PART), f32),
            shape((SLOTS, LEAF), i32),
            shape((1, LEAF), i32),
        ] + work,
        in_specs=[HB] * 5,
        out_specs=[VM] * 4 + [SM] + [VM] * 5,
        scratch_shapes=[gather_room, pltpu.SemaphoreType.DMA((12,))] + product_room + list_room,
        compiler_params=PARAMS,
        name="front",
    )(*fixed[:5])
    moved = [lax.ppermute(edge, "bit", [(i, i ^ (1 << n)) for i in range(bits)]) for n in (0, 3, 4, 1, 2)]
    beside = {i: i + 1 for i in range(1, sects - 1, 2)}
    beside.update({j: i for i, j in beside.items()})
    pairs = [
        (b * sects + i, b * sects + beside[i] if i in beside else (b ^ 1) * sects + i)
        for b in range(bits) for i in range(sects)
    ]
    moved.append(lax.ppermute(edge, ("bit", "sect"), pairs))
    moved.append(lax.ppermute(edge, "sect", [(i, i ^ 1) for i in range(sects)]))
    z1, y1, y2, z2, z4, outer, inner = moved
    notes1, centres, table, acc = pl.pallas_call(
        local_kernel,
        out_shape=[work[n] for n in (0, 1, 2, 5)],
        in_specs=[SM] + [VM] * 8,
        out_specs=[SM] + [VM] * 3,
        scratch_shapes=[gather_room] + source_room + product_room + list_room,
        compiler_params=PARAMS,
        name="local_pairs",
    )(notes0, near, counts, own, *held)
    return pl.pallas_call(
        remote_kernel,
        out_shape=[shape((3, LEAF, PART), f32)] * 2,
        in_specs=[SM, SM] + [VM] * 4 + [HB] + [VM] * 7,
        out_specs=[VM, VM],
        scratch_shapes=[
            pltpu.VMEM((12, LEAF), f32),
            gather_room,
            *source_room,
            *product_room,
            pltpu.VMEM((2 * SUMS, PART), f32),
            pltpu.SMEM((ROOM,), i32),
            pltpu.SemaphoreType.DMA((1,)),
        ],
        compiler_params=PARAMS,
        name="remote_pairs",
    )(notes0, notes1, own, centres, table, acc, fixed[5], z1, y1, y2, z2, z4, outer, inner)


def solution(mesh):
    in_specs = (
        P(None, ("bit", "sect"), None),
        P(None, ("bit", "sect"), None),
        P(("bit", "sect"), None),
        P(None, ("bit", "sect")),
        P(("bit", "sect"), None),
        P(("bit", "sect")),
    )
    out_specs = (P(None, ("bit", "sect"), None), P(None, ("bit", "sect"), None))
    return jax.shard_map(body, mesh=mesh, in_specs=in_specs, out_specs=out_specs, check_vma=False)
```

```python
import math

import jax
import jax.numpy as jnp
from jax import lax
from jax.experimental import pallas as pl
from jax.experimental.pallas import tpu as pltpu
from jax.sharding import PartitionSpec as P

inv_four_pi = 1.0 / (4.0 * math.pi)
f32, bf16, i32 = jnp.float32, jnp.bfloat16, jnp.int32

LEAF = 32
PART = 128
SLOTS = 8
EDGE = 24
FIELDS = 7
MOVED = FIELDS * EDGE
PAIRS = LEAF * SLOTS
BATCH = 16
HALF = BATCH // 2
ROOM = PAIRS + 2 * BATCH
TABLE = (LEAF + 1) * 32
SUMS = (LEAF + 1) * 16


def rounded(value):
    return value.astype(bf16).astype(f32)


def split3(value):
    high = rounded(value)
    rest = value - high
    mid = rounded(rest)
    return high, mid, rest - mid


def split2(value):
    high = value.astype(bf16)
    return high, (value - high.astype(f32)).astype(bf16)


def leaf_fields(own, group, fields):
    return [own[pl.ds(k * LEAF + group * 8, 8), :] for k in fields]


def offsets(own, group):
    point = leaf_fields(own, group, range(3))
    centre = [jnp.mean(v, axis=1, keepdims=True) for v in point]
    return centre, [v - c for v, c in zip(point, centre)]


def build_targets(own, centres, table, stage):
    for group in range(LEAF // 8):
        centre, off = offsets(own, group)
        a = leaf_fields(own, group, range(3, 6))
        zero = jnp.zeros((8, PART), f32)
        one = jnp.ones((8, PART), f32)
        for k in range(8):
            row = jnp.broadcast_to(centre[k], (8, PART)) if k < 3 else zero
            centres[pl.ds(group * 64 + k, 8, stride=8), :] = row
        left = [split3(-2.0 * v) for v in off]
        right = [split3(-v) for v in a]
        square = split3(off[0] * off[0] + off[1] * off[1] + off[2] * off[2])
        along = split3(off[0] * a[0] + off[1] * a[1] + off[2] * a[2])
        rows = []
        for part in (0, 1, 2, 0, 1, 0):
            rows += [(left[k][part], right[k][part]) for k in range(3)]
        rows += [(one, zero)] * 3
        rows += [(square[k], along[k]) for k in range(3)]
        rows += [(zero, zero)] * 8
        for k, (spread_row, proj_row) in enumerate(rows):
            stage[pl.ds(group * 512 + k, 8, stride=32), :] = spread_row
            stage[pl.ds(group * 512 + 256 + k, 8, stride=32), :] = proj_row
        for side in range(2):
            table[pl.ds(side * TABLE + group * 256, 256), :] = stage[
                pl.ds(group * 512 + side * 256, 256), :
            ].astype(bf16)


def source_rows(gathered, left, right, group):
    first = pl.multiple_of(group * 64, 64)
    q = [gathered[pl.ds(first + k, 8, stride=8), :] for k in range(FIELDS)]
    x, a, core = q[:3], q[3:6], q[6]
    part = [split3(v) for v in x]
    size = split3(x[0] * x[0] + x[1] * x[1] + x[2] * x[2] + core * core)
    one = jnp.ones((8, PART), f32)
    rows = []
    for level in (0, 0, 0, 1, 1, 2):
        rows += [part[k][level] for k in range(3)]
    rows += list(size) + [one] * 3
    base = pl.multiple_of(group * 192, 64)
    for k, row in enumerate(rows):
        left[pl.ds(base + k, 8, stride=24), :] = row
    crossed = [
        x[1] * a[2] - x[2] * a[1],
        x[2] * a[0] - x[0] * a[2],
        x[0] * a[1] - x[1] * a[0],
    ]
    base = pl.multiple_of(group * 128, 128)
    for k, row in enumerate(a + crossed):
        high = rounded(row)
        right[pl.ds(base + k, 8, stride=16), :] = high
        right[pl.ds(base + 6 + k, 8, stride=16), :] = row - high
    for k in range(12, 16):
        right[pl.ds(base + k, 8, stride=16), :] = jnp.zeros((8, PART), f32)


def pair_products(pair, target, table, left):
    lhs = left[pl.ds(pl.multiple_of(pair * 24, 8), 24), :]
    lhs = jnp.concatenate([lhs, jnp.zeros((8, PART), f32)], axis=0).astype(bf16)
    first = pl.multiple_of(target * 32, 32)
    rhs = jnp.concatenate([table[pl.ds(first, 32), :], table[pl.ds(TABLE + first, 32), :]], axis=1)
    return lax.dot_general(lhs, rhs, (((0,), (0,)), ((), ())), preferred_element_type=f32)


def pair_total(pair, both, right):
    spread, proj = both[:, :PART], both[:, PART:]
    root = lax.rsqrt(spread)
    square = root * root
    kernel = root * square
    weight = kernel * square * proj
    k_high, k_low = split2(kernel)
    w_high, w_low = split2(weight)
    pairs = jnp.concatenate(
        [jnp.concatenate([k_high, w_high], axis=1), jnp.concatenate([k_low, w_low], axis=1)], axis=0
    )
    rows = right[pl.ds(pl.multiple_of(pair * 16, 16), 16), :].astype(bf16)
    rows = jnp.concatenate([rows, rows], axis=1)
    return jnp.dot(rows, pairs, preferred_element_type=f32)


def half_batch(begin, now, later, target_of, table, left, right, acc, carry):
    last, total = carry
    results = []
    for lane in range(HALF):
        pair = begin + lane
        ahead = pair + HALF
        later[lane] = pair_products(ahead, target_of[ahead], table, left)
        results.append((target_of[pair], pair_total(pair, now[lane], right)))
    for target, value in results:
        total = jnp.where(target == last, total, 0.0) + value
        last = target
        first = pl.multiple_of(target * 16, 16)
        for side in range(2):
            acc[pl.ds(side * SUMS + first, 16), :] = total[:, side * PART : (side + 1) * PART]
    return last, total


def features(count, gathered, left, right):
    lax.fori_loop(0, (count + 7) // 8, lambda g, c: (source_rows(gathered, left, right, g), c)[1], 0)


def sum_pairs(begin, end, target_of, table, left, right, acc, products, carry):
    even, odd = products
    work = (target_of, table, left, right, acc)

    @pl.when(begin < end)
    def _():
        for lane in range(HALF):
            pair = begin * BATCH + lane
            even[lane] = pair_products(pair, target_of[pair], table, left)

    def step(s, c):
        c = half_batch(s * BATCH, even, odd, *work, c)
        return half_batch(s * BATCH + HALF, odd, even, *work, c)

    lax.fori_loop(begin, end, step, carry)


def start_carry():
    return jnp.int32(-1), jnp.zeros((16, 2 * PART), f32)


def batches(count):
    return (count + BATCH - 1) // BATCH


def slot_codes(near, counts):
    slot = lax.broadcasted_iota(i32, near.shape, 0)
    used = slot < counts
    times = jnp.ones(near.shape, i32)
    fresh = used
    for d in range(1, SLOTS):
        after = pltpu.roll(near, SLOTS - d, 0)
        times = times + ((after == near) & (slot + d < counts)).astype(i32)
        before = pltpu.roll(near, d, 0)
        fresh = fresh & ~((before == near) & (slot >= d))
    owner = near >> 5
    me = jnp.broadcast_to(near[0:1, 0:1] >> 5, near.shape)
    differs = owner ^ me
    bit = differs >> 3
    part = jnp.where(bit == 0, jnp.where(differs == 1, 0, 1), 2)
    for n in range(1, 5):
        part = jnp.where(bit == 1 << n, 2 + n, part)
    mine = differs == 0
    code = jnp.where(mine, 1, 2) + times * 4 + (part * LEAF + (near & (LEAF - 1))) * 64
    return jnp.where(fresh, code, 0)


def early_leaves(codes):
    z = lax.axis_index("bit") & 7
    local = (codes & 1).astype(f32)
    row = lax.broadcasted_iota(i32, (LEAF, LEAF), 0)
    upto = (row <= lax.broadcasted_iota(i32, (LEAF, LEAF), 1)).astype(f32)
    held = jnp.sum(jnp.dot(local, upto, preferred_element_type=f32), axis=0, keepdims=True)
    count = jnp.sum(local).astype(i32)
    ahead = jnp.minimum(jnp.maximum(batches(count) - 2 - z, 0), 5) * BATCH
    leaves = jnp.sum((held <= ahead.astype(f32)).astype(f32)).astype(i32)
    return jnp.where((z < 2) & (ahead > 0), leaves, 0)


def early_codes(codes, leaves):
    return (codes & 1 == 1) & (lax.broadcasted_iota(i32, codes.shape, 1) < leaves)


def scaled(source, centre, code):
    row = lax.broadcasted_iota(i32, (FIELDS, PART), 0)
    found = source - centre
    return jnp.where((row >= 3) & (row < 6), found * ((code >> 2) & 15).astype(f32), found)


def scan(leaves, codes, own, centres, gathered, targets, remote):
    def leaf(t, carry):
        place, outside = carry
        centre = centres[pl.ds(pl.multiple_of(t * 8, 8), 8), :][:FIELDS]
        for slot in range(SLOTS):
            code = codes[slot, t]
            source = own[pl.ds((code >> 6) & (LEAF - 1), FIELDS, stride=LEAF), :]
            gathered[pl.ds(pl.multiple_of(place * 8, 8), FIELDS), :] = scaled(source, centre, code)
            targets[place] = t
            place = place + (code & 1)
            if remote is not None:
                remote[outside] = (t << 20) | code
                outside = outside + ((code >> 1) & 1)
        return place, outside

    count, outside = lax.fori_loop(0, leaves, leaf, (jnp.int32(0), jnp.int32(0)))
    if remote is not None:
        remote[PAIRS + 1] = outside
    close_list(targets, count)
    return count


def close_list(targets, count):
    for lane in range(2 * BATCH):
        targets[count + lane] = LEAF


def fetched(codes, codes_s, sem):
    fetch = pltpu.make_async_copy(codes, codes_s, sem.at[0])
    fetch.start()
    return fetch


def front_kernel(pos, stren, cores, near, counts, own, edge, near_v, counts_v, acc,
                 gathered, sems, left, right, even, odd, stage, centres, table, targets, codes, codes_s, sem):
    copies = []
    for k in range(FIELDS):
        ref, base = ((pos, k), (stren, k - 3), (cores, 0))[min(k // 3, 2)]
        copies.append((ref.at[pl.ds(base * LEAF, EDGE)], edge.at[pl.ds(k * EDGE, EDGE)]))
    copies += [
        (pos, own.at[pl.ds(0, 96)]),
        (stren, own.at[pl.ds(96, 96)]),
        (cores, own.at[pl.ds(192, 32)]),
        (near, near_v),
        (counts, counts_v),
    ]
    copies = [pltpu.make_async_copy(a, b, sems.at[n]) for n, (a, b) in enumerate(copies)]
    for copy in copies:
        copy.start()
    acc[...] = jnp.zeros_like(acc)
    for copy in copies:
        copy.wait()

    @pl.when(lax.axis_index("bit") & 7 < 2)
    def _():
        found = slot_codes(near_v[...], counts_v[...])
        leaves = early_leaves(found)

        @pl.when(leaves > 0)
        def _():
            codes[...] = jnp.where(early_codes(found, leaves), found, 0)
            fetch = fetched(codes, codes_s, sem)
            build_targets(own, centres, table, stage)
            fetch.wait()
            count = scan(leaves, codes_s, own, centres, gathered, targets, None)
            features(count, gathered, left, right)
            sum_pairs(0, batches(count), targets, table, left, right, acc, (even, odd), start_carry())


def local_kernel(near, counts, own, remote, acc, centres, table,
                 gathered, left, right, even, odd, stage, targets, codes, codes_s, sem):
    found = slot_codes(near[...], counts[...])
    codes[...] = found

    @pl.when(lax.axis_index("bit") & 7 < 2)
    def _():
        codes[...] = jnp.where(early_codes(found, early_leaves(found)), 0, found)

    fetch = fetched(codes, codes_s, sem)
    build_targets(own, centres, table, stage)
    acc[...] = jnp.zeros_like(acc)
    fetch.wait()
    count = scan(LEAF, codes_s, own, centres, gathered, targets, remote)
    features(count, gathered, left, right)
    sum_pairs(0, batches(count), targets, table, left, right, acc, (even, odd), start_carry())


def remote_kernel(remote, own, centres, table, acc0, acc1, far, p1, p8, p16, p2, p4, outer_part, inner_part,
                  velocity, stretching, far_v, sem, gathered, left, right, even, odd, targets, acc):
    parts = (inner_part, outer_part, p1, p2, p4, p8, p16)
    copy = pltpu.make_async_copy(far, far_v, sem.at[0])
    copy.start()
    acc[...] = jnp.zeros_like(acc)
    count = remote[PAIRS + 1]

    def one(n, _):
        code = remote[n]
        target = code >> 20
        where = pl.ds((code >> 6) & (LEAF - 1), FIELDS, stride=EDGE)
        part = (code >> 11) & 7
        source = parts[0][where, :]
        for k in range(1, 7):
            source = jnp.where(part == k, parts[k][where, :], source)
        centre = centres[pl.ds(pl.multiple_of(target * 8, 8), 8), :][:FIELDS]
        gathered[pl.ds(pl.multiple_of(n * 8, 8), FIELDS), :] = scaled(source, centre, code)
        targets[n] = target
        return 0

    lax.fori_loop(0, count, one, 0)
    close_list(targets, count)
    features(count, gathered, left, right)
    sum_pairs(0, batches(count), targets, table, left, right, acc, (even, odd), start_carry())
    copy.wait()

    coefs = far_v[...].T
    for group in range(LEAF // 8):
        rows = pl.ds(group * 8, 8)
        _, off = offsets(own, group)
        a = leaf_fields(own, group, range(3, 6))

        def summed(field, side):
            first = side * SUMS + group * 128 + field
            parts = [
                ref[pl.ds(first + low, 8, stride=16), :] for ref in (acc0, acc1, acc) for low in (0, 6)
            ]
            return (parts[0] + parts[1]) + (parts[2] + parts[3]) + (parts[4] + parts[5])

        ka = [summed(k, 0) for k in range(3)]
        kc = [summed(3 + k, 0) for k in range(3)]
        wa = [summed(k, 1) for k in range(3)]
        wc = [summed(3 + k, 1) for k in range(3)]
        coef = [coefs[group * 8 : group * 8 + 8, k : k + 1] for k in range(12)]
        for i in range(3):
            j, k = (i + 1) % 3, (i + 2) % 3
            near_vel = off[j] * ka[k] - off[k] * ka[j] - kc[i]
            steep = off[j] * wa[k] - off[k] * wa[j] - wc[i]
            near_str = a[j] * ka[k] - a[k] * ka[j] - 3.0 * steep
            grad = [coef[3 + 3 * i + m] for m in range(3)]
            velocity[i, rows, :] = (
                -inv_four_pi * near_vel + coef[i]
                + grad[0] * off[0] + grad[1] * off[1] + grad[2] * off[2]
            )
            stretching[i, rows, :] = (
                -inv_four_pi * near_str + grad[0] * a[0] + grad[1] * a[1] + grad[2] * a[2]
            )


VM = pl.BlockSpec(memory_space=pltpu.VMEM)
SM = pl.BlockSpec(memory_space=pltpu.SMEM)
HB = pl.BlockSpec(memory_space=pltpu.HBM)
PARAMS = pltpu.CompilerParams(vmem_limit_bytes=24 * 2**20)


def body(positions, strengths, cores, far_coef, near_list, near_count):
    bits, sects = lax.axis_size("bit"), lax.axis_size("sect")
    shape = jax.ShapeDtypeStruct
    source_room = [pltpu.VMEM((ROOM * 24, PART), f32), pltpu.VMEM((ROOM * 16, PART), f32)]
    pair_room = source_room + [pltpu.VMEM((HALF, PART, 2 * PART), f32)] * 2
    stage_room = pltpu.VMEM((2048, PART), f32)
    target_room = [pltpu.VMEM((LEAF * 8, PART), f32), pltpu.VMEM((2 * TABLE, PART), bf16)]
    list_room = [
        pltpu.SMEM((ROOM,), i32),
        pltpu.VMEM((SLOTS, LEAF), i32),
        pltpu.SMEM((SLOTS, LEAF), i32),
        pltpu.SemaphoreType.DMA((1,)),
    ]
    gather_room = pltpu.VMEM((ROOM * 8, PART), f32)
    sums = (2 * SUMS, PART)
    fixed = [
        pltpu.with_memory_space_constraint(v, pltpu.HBM)
        for v in (
            positions.reshape(3 * LEAF, PART),
            strengths.reshape(3 * LEAF, PART),
            cores,
            near_list.T,
            near_count.reshape(1, LEAF),
            far_coef,
        )
    ]
    own, edge, near, counts, acc0 = pl.pallas_call(
        front_kernel,
        out_shape=[
            shape((LEAF * FIELDS, PART), f32),
            shape((MOVED, PART), f32),
            shape((SLOTS, LEAF), i32),
            shape((1, LEAF), i32),
            shape(sums, f32),
        ],
        in_specs=[HB] * 5,
        out_specs=[VM] * 5,
        scratch_shapes=[gather_room, pltpu.SemaphoreType.DMA((12,))] + pair_room + [stage_room]
        + target_room + list_room,
        compiler_params=PARAMS,
        name="front",
    )(*fixed[:5])
    moved = [lax.ppermute(edge, "bit", [(i, i ^ (1 << n)) for i in range(bits)]) for n in (0, 3, 4, 1, 2)]
    beside = {i: i + 1 for i in range(1, sects - 1, 2)}
    beside.update({j: i for i, j in beside.items()})
    pairs = [
        (b * sects + i, b * sects + beside[i] if i in beside else (b ^ 1) * sects + i)
        for b in range(bits) for i in range(sects)
    ]
    moved.append(lax.ppermute(edge, ("bit", "sect"), pairs))
    moved.append(lax.ppermute(edge, "sect", [(i, i ^ 1) for i in range(sects)]))
    z1, y1, y2, z2, z4, outer, inner = moved
    remote, acc1, centres, table = pl.pallas_call(
        local_kernel,
        out_shape=[
            shape((PAIRS + 8,), i32),
            shape(sums, f32),
            shape((LEAF * 8, PART), f32),
            shape((2 * TABLE, PART), bf16),
        ],
        in_specs=[VM] * 3,
        out_specs=[SM] + [VM] * 3,
        scratch_shapes=[gather_room] + pair_room + [stage_room] + list_room,
        compiler_params=PARAMS,
        name="local_pairs",
    )(near, counts, own)
    return pl.pallas_call(
        remote_kernel,
        out_shape=[shape((3, LEAF, PART), f32)] * 2,
        in_specs=[SM] + [VM] * 5 + [HB] + [VM] * 7,
        out_specs=[VM, VM],
        scratch_shapes=[pltpu.VMEM((12, LEAF), f32), pltpu.SemaphoreType.DMA((1,)), gather_room] + pair_room
        + [list_room[0], pltpu.VMEM(sums, f32)],
        compiler_params=PARAMS,
        name="remote_pairs",
    )(remote, own, centres, table, acc0, acc1, fixed[5], z1, y1, y2, z2, z4, outer, inner)


def solution(mesh):
    in_specs = (
        P(None, ("bit", "sect"), None),
        P(None, ("bit", "sect"), None),
        P(("bit", "sect"), None),
        P(None, ("bit", "sect")),
        P(("bit", "sect"), None),
        P(("bit", "sect")),
    )
    out_specs = (P(None, ("bit", "sect"), None), P(None, ("bit", "sect"), None))
    return jax.shard_map(body, mesh=mesh, in_specs=in_specs, out_specs=out_specs, check_vma=False)
```

```python
import math

import jax
import jax.numpy as jnp
from jax import lax
from jax.experimental import pallas as pl
from jax.experimental.pallas import tpu as pltpu
from jax.sharding import PartitionSpec as P

inv_four_pi = 1.0 / (4.0 * math.pi)
f32, bf16, i32 = jnp.float32, jnp.bfloat16, jnp.int32

LEAF = 32
PART = 128
SLOTS = 8
EDGE = 24
FIELDS = 7
MOVED = FIELDS * EDGE
PAIRS = LEAF * SLOTS
BATCH = 24
HALF = BATCH // 2
ROOM = PAIRS + 2 * BATCH
TABLE = (LEAF + 1) * 32
SUMS = (LEAF + 1) * 16


def rounded(value):
    return value.astype(bf16).astype(f32)


def split3(value):
    high = rounded(value)
    rest = value - high
    mid = rounded(rest)
    return high, mid, rest - mid


def split2(value):
    high = value.astype(bf16)
    return high, (value - high.astype(f32)).astype(bf16)


def leaf_fields(own, group, fields):
    return [own[pl.ds(k * LEAF + group * 8, 8), :] for k in fields]


def offsets(own, group):
    point = leaf_fields(own, group, range(3))
    centre = [jnp.mean(v, axis=1, keepdims=True) for v in point]
    return centre, [v - c for v, c in zip(point, centre)]


def build_targets(own, centres, table, stage):
    for group in range(LEAF // 8):
        centre, off = offsets(own, group)
        a = leaf_fields(own, group, range(3, 6))
        zero = jnp.zeros((8, PART), f32)
        one = jnp.ones((8, PART), f32)
        for k in range(8):
            row = jnp.broadcast_to(centre[k], (8, PART)) if k < 3 else zero
            centres[pl.ds(group * 64 + k, 8, stride=8), :] = row
        left = [split3(-2.0 * v) for v in off]
        right = [split3(-v) for v in a]
        square = split3(off[0] * off[0] + off[1] * off[1] + off[2] * off[2])
        along = split3(off[0] * a[0] + off[1] * a[1] + off[2] * a[2])
        rows = []
        level = [[(left[k][part], right[k][part]) for k in range(3)] for part in range(3)]
        rows += level[0] * 2 + [(one, zero)] * 2
        rows += level[0] + [(one, zero)] + [(square[k], along[k]) for k in range(3)] + [(zero, zero)]
        rows += level[1] * 2 + [(zero, zero)] * 2
        rows += level[2] * 2 + [(zero, zero)] * 2
        for k, (spread_row, proj_row) in enumerate(rows):
            stage[pl.ds(group * 512 + k, 8, stride=32), :] = spread_row
            stage[pl.ds(group * 512 + 256 + k, 8, stride=32), :] = proj_row
        for side in range(2):
            table[pl.ds(side * TABLE + group * 256, 256), :] = stage[
                pl.ds(group * 512 + side * 256, 256), :
            ].astype(bf16)


def source_rows(gathered, left, right, group):
    first = pl.multiple_of(group * 64, 64)
    q = [gathered[pl.ds(first + k, 8, stride=8), :] for k in range(FIELDS)]
    x, a, core = q[:3], q[3:6], q[6]
    part = [split3(v) for v in x]
    size = split3(x[0] * x[0] + x[1] * x[1] + x[2] * x[2] + core * core)
    one = jnp.ones((8, PART), f32)
    rows = [part[k][level] for level in (0, 1) for k in range(3)] + [size[0], size[1]]
    rows += [part[k][2] for k in range(3)] + [size[2]] + [one] * 4
    base = pl.multiple_of(group * 128, 128)
    for k, row in enumerate(rows):
        left[pl.ds(base + k, 8, stride=16), :] = row
    crossed = [
        x[1] * a[2] - x[2] * a[1],
        x[2] * a[0] - x[0] * a[2],
        x[0] * a[1] - x[1] * a[0],
    ]
    for k, row in enumerate(a + crossed):
        high = rounded(row)
        right[pl.ds(base + k, 8, stride=16), :] = high
        right[pl.ds(base + 6 + k, 8, stride=16), :] = row - high


def pair_products(pair, target, table, left):
    rows = left[pl.ds(pl.multiple_of(pair * 16, 16), 16), :]
    lhs = jnp.concatenate([rows, rows[:8], rows[:8]], axis=0).astype(bf16)
    first = pl.multiple_of(target * 32, 32)
    rhs = jnp.concatenate([table[pl.ds(first, 32), :], table[pl.ds(TABLE + first, 32), :]], axis=1)
    return lax.dot_general(lhs, rhs, (((0,), (0,)), ((), ())), preferred_element_type=f32)


def pair_total(pair, both, right):
    spread, proj = both[:, :PART], both[:, PART:]
    root = lax.rsqrt(spread)
    square = root * root
    kernel = root * square
    weight = kernel * square * proj
    k_high, k_low = split2(kernel)
    w_high, w_low = split2(weight)
    pairs = jnp.concatenate(
        [jnp.concatenate([k_high, w_high], axis=1), jnp.concatenate([k_low, w_low], axis=1)], axis=0
    )
    rows = right[pl.ds(pl.multiple_of(pair * 16, 16), 16), :].astype(bf16)
    rows = jnp.concatenate([rows, rows], axis=1)
    return jnp.dot(rows, pairs, preferred_element_type=f32)


def half_batch(begin, now, later, target_of, table, left, right, acc, carry):
    last, total = carry
    results = []
    for lane in range(HALF):
        pair = begin + lane
        if later is not None:
            ahead = pair + HALF
            later[lane] = pair_products(ahead, target_of[ahead], table, left)
        results.append((target_of[pair], pair_total(pair, now[lane], right)))
    for target, value in results:
        total = jnp.where(target == last, total, 0.0) + value
        last = target
        first = pl.multiple_of(target * 16, 16)
        for side in range(2):
            acc[pl.ds(side * SUMS + first, 16), :] = total[:, side * PART : (side + 1) * PART]
    return last, total


def features(count, gathered, left, right):
    def two(step, _):
        source_rows(gathered, left, right, 2 * step)
        source_rows(gathered, left, right, 2 * step + 1)
        return 0

    lax.fori_loop(0, (count + 15) // 16, two, 0)


def sum_pairs(count, target_of, table, left, right, acc, products):
    even, odd = products
    work = (target_of, table, left, right, acc)
    halves = (count + HALF - 1) // HALF

    @pl.when(count > 0)
    def _():
        for lane in range(HALF):
            even[lane] = pair_products(lane, target_of[lane], table, left)

    def step(s, c):
        c = half_batch(s * BATCH, even, odd, *work, c)
        return half_batch(s * BATCH + HALF, odd, even, *work, c)

    carry = (jnp.int32(-1), jnp.zeros((16, 2 * PART), f32))
    carry = lax.fori_loop(0, halves // 2, step, carry)

    @pl.when(halves & 1 == 1)
    def _():
        half_batch((halves - 1) * HALF, even, None, *work, carry)


def slot_codes(near, counts):
    slot = lax.broadcasted_iota(i32, near.shape, 0)
    used = slot < counts
    times = jnp.ones(near.shape, i32)
    fresh = used
    for d in range(1, SLOTS):
        after = pltpu.roll(near, SLOTS - d, 0)
        times = times + ((after == near) & (slot + d < counts)).astype(i32)
        before = pltpu.roll(near, d, 0)
        fresh = fresh & ~((before == near) & (slot >= d))
    owner = near >> 5
    me = jnp.broadcast_to(near[0:1, 0:1] >> 5, near.shape)
    differs = owner ^ me
    bit = differs >> 3
    part = jnp.where(bit == 0, jnp.where(differs == 1, 0, 1), 2)
    for n in range(1, 5):
        part = jnp.where(bit == 1 << n, 2 + n, part)
    mine = differs == 0
    target = lax.broadcasted_iota(i32, near.shape, 1)
    code = jnp.where(mine, 1, 2) + times * 4 + target * 64 + part * 2048 + (near & (LEAF - 1)) * 16384
    return jnp.where(fresh, code, 0)


def early_leaves(codes):
    z = lax.axis_index("bit") & 7
    local = (codes & 1).astype(f32)
    row = lax.broadcasted_iota(i32, (LEAF, LEAF), 0)
    upto = (row <= lax.broadcasted_iota(i32, (LEAF, LEAF), 1)).astype(f32)
    held = jnp.sum(jnp.dot(local, upto, preferred_element_type=f32), axis=0, keepdims=True)
    count = jnp.sum(local).astype(i32)
    ahead = jnp.minimum(jnp.maximum(count - 16 * (z + 2), 0), 80)
    leaves = jnp.sum((held <= ahead.astype(f32)).astype(f32)).astype(i32)
    return jnp.where((z < 2) & (ahead > 0), leaves, 0)


def early_codes(codes, leaves):
    return (codes & 1 == 1) & (lax.broadcasted_iota(i32, codes.shape, 1) < leaves)


def scaled(source, centre, code):
    row = lax.broadcasted_iota(i32, (FIELDS, PART), 0)
    found = source - centre
    return jnp.where((row >= 3) & (row < 6), found * ((code >> 2) & 15).astype(f32), found)


def scan(leaves, codes, own, centres, gathered, targets, remote):
    def leaf(t, carry):
        place, outside = carry
        centre = centres[pl.ds(pl.multiple_of(t * 8, 8), 8), :][:FIELDS]
        for slot in range(SLOTS):
            code = codes[slot, t]
            source = own[pl.ds(code >> 14, FIELDS, stride=LEAF), :]
            gathered[pl.ds(pl.multiple_of(place * 8, 8), FIELDS), :] = scaled(source, centre, code)
            targets[place] = t
            place = place + (code & 1)
            if remote is not None:
                remote[outside] = code
                outside = outside + ((code >> 1) & 1)
        return place, outside

    count, outside = lax.fori_loop(0, leaves, leaf, (jnp.int32(0), jnp.int32(0)))
    if remote is not None:
        for k in range(3):
            remote[outside + k] = 0
        remote[PAIRS + 7] = outside
    close_list(targets, count)
    return count


def close_list(targets, count):
    for lane in range(2 * BATCH):
        targets[count + lane] = LEAF


def fetched(codes, codes_s, sem):
    fetch = pltpu.make_async_copy(codes, codes_s, sem.at[0])
    fetch.start()
    return fetch


def front_kernel(pos, stren, cores, near, counts, own, edge, near_v, counts_v, acc,
                 gathered, sems, left, right, even, odd, stage, centres, table, targets, codes, codes_s, sem):
    copies = []
    for k in range(FIELDS):
        ref, base = ((pos, k), (stren, k - 3), (cores, 0))[min(k // 3, 2)]
        copies.append((ref.at[pl.ds(base * LEAF, EDGE)], edge.at[pl.ds(k * EDGE, EDGE)]))
    copies += [
        (pos, own.at[pl.ds(0, 96)]),
        (stren, own.at[pl.ds(96, 96)]),
        (cores, own.at[pl.ds(192, 32)]),
        (near, near_v),
        (counts, counts_v),
    ]
    copies = [pltpu.make_async_copy(a, b, sems.at[n]) for n, (a, b) in enumerate(copies)]
    for copy in copies:
        copy.start()
    acc[...] = jnp.zeros_like(acc)
    for copy in copies:
        copy.wait()

    @pl.when(lax.axis_index("bit") & 7 < 2)
    def _():
        found = slot_codes(near_v[...], counts_v[...])
        leaves = early_leaves(found)

        @pl.when(leaves > 0)
        def _():
            codes[...] = jnp.where(early_codes(found, leaves), found, 0)
            fetch = fetched(codes, codes_s, sem)
            build_targets(own, centres, table, stage)
            fetch.wait()
            count = scan(leaves, codes_s, own, centres, gathered, targets, None)
            features(count, gathered, left, right)
            sum_pairs(count, targets, table, left, right, acc, (even, odd))


def local_kernel(near, counts, own, remote, acc, centres, table,
                 gathered, left, right, even, odd, stage, targets, codes, codes_s, sem):
    found = slot_codes(near[...], counts[...])
    codes[...] = found

    @pl.when(lax.axis_index("bit") & 7 < 2)
    def _():
        codes[...] = jnp.where(early_codes(found, early_leaves(found)), 0, found)

    fetch = fetched(codes, codes_s, sem)
    build_targets(own, centres, table, stage)
    acc[...] = jnp.zeros_like(acc)
    fetch.wait()
    count = scan(LEAF, codes_s, own, centres, gathered, targets, remote)
    features(count, gathered, left, right)
    sum_pairs(count, targets, table, left, right, acc, (even, odd))


def remote_kernel(remote, own, centres, table, acc0, acc1, far, p1, p8, p16, p2, p4, outer_part, inner_part,
                  velocity, stretching, far_v, sem, gathered, left, right, even, odd, targets, acc):
    parts = (inner_part, outer_part, p1, p2, p4, p8, p16)
    copy = pltpu.make_async_copy(far, far_v, sem.at[0])
    copy.start()
    acc[...] = jnp.zeros_like(acc)
    count = remote[PAIRS + 7]

    def four(step, _):
        for lane in range(4):
            n = step * 4 + lane
            code = remote[n]
            target = (code >> 6) & (LEAF - 1)
            where = pl.ds(code >> 14, FIELDS, stride=EDGE)
            part = (code >> 11) & 7
            source = parts[0][where, :]
            for k in range(1, 7):
                source = jnp.where(part == k, parts[k][where, :], source)
            centre = centres[pl.ds(pl.multiple_of(target * 8, 8), 8), :][:FIELDS]
            gathered[pl.ds(pl.multiple_of(n * 8, 8), FIELDS), :] = scaled(source, centre, code)
            targets[n] = target
        return 0

    lax.fori_loop(0, (count + 3) // 4, four, 0)
    close_list(targets, count)
    features(count, gathered, left, right)
    sum_pairs(count, targets, table, left, right, acc, (even, odd))
    copy.wait()

    coefs = far_v[...].T
    for group in range(LEAF // 8):
        rows = pl.ds(group * 8, 8)
        _, off = offsets(own, group)
        a = leaf_fields(own, group, range(3, 6))

        def summed(field, side):
            first = side * SUMS + group * 128 + field
            parts = [
                ref[pl.ds(first + low, 8, stride=16), :] for ref in (acc0, acc1, acc) for low in (0, 6)
            ]
            return (parts[0] + parts[1]) + (parts[2] + parts[3]) + (parts[4] + parts[5])

        ka = [summed(k, 0) for k in range(3)]
        kc = [summed(3 + k, 0) for k in range(3)]
        wa = [summed(k, 1) for k in range(3)]
        wc = [summed(3 + k, 1) for k in range(3)]
        coef = [coefs[group * 8 : group * 8 + 8, k : k + 1] for k in range(12)]
        for i in range(3):
            j, k = (i + 1) % 3, (i + 2) % 3
            near_vel = off[j] * ka[k] - off[k] * ka[j] - kc[i]
            steep = off[j] * wa[k] - off[k] * wa[j] - wc[i]
            near_str = a[j] * ka[k] - a[k] * ka[j] - 3.0 * steep
            grad = [coef[3 + 3 * i + m] for m in range(3)]
            velocity[i, rows, :] = (
                -inv_four_pi * near_vel + coef[i]
                + grad[0] * off[0] + grad[1] * off[1] + grad[2] * off[2]
            )
            stretching[i, rows, :] = (
                -inv_four_pi * near_str + grad[0] * a[0] + grad[1] * a[1] + grad[2] * a[2]
            )


VM = pl.BlockSpec(memory_space=pltpu.VMEM)
SM = pl.BlockSpec(memory_space=pltpu.SMEM)
HB = pl.BlockSpec(memory_space=pltpu.HBM)
PARAMS = pltpu.CompilerParams(vmem_limit_bytes=24 * 2**20)


def body(positions, strengths, cores, far_coef, near_list, near_count):
    bits, sects = lax.axis_size("bit"), lax.axis_size("sect")
    shape = jax.ShapeDtypeStruct
    source_room = [pltpu.VMEM((ROOM * 16, PART), f32), pltpu.VMEM((ROOM * 16, PART), f32)]
    pair_room = source_room + [pltpu.VMEM((HALF, PART, 2 * PART), f32)] * 2
    stage_room = pltpu.VMEM((2048, PART), f32)
    target_room = [pltpu.VMEM((LEAF * 8, PART), f32), pltpu.VMEM((2 * TABLE, PART), bf16)]
    list_room = [
        pltpu.SMEM((ROOM,), i32),
        pltpu.VMEM((SLOTS, LEAF), i32),
        pltpu.SMEM((SLOTS, LEAF), i32),
        pltpu.SemaphoreType.DMA((1,)),
    ]
    gather_room = pltpu.VMEM((ROOM * 8, PART), f32)
    sums = (2 * SUMS, PART)
    fixed = [
        pltpu.with_memory_space_constraint(v, pltpu.HBM)
        for v in (
            positions.reshape(3 * LEAF, PART),
            strengths.reshape(3 * LEAF, PART),
            cores,
            near_list.T,
            near_count.reshape(1, LEAF),
            far_coef,
        )
    ]
    own, edge, near, counts, acc0 = pl.pallas_call(
        front_kernel,
        out_shape=[
            shape((LEAF * FIELDS, PART), f32),
            shape((MOVED, PART), f32),
            shape((SLOTS, LEAF), i32),
            shape((1, LEAF), i32),
            shape(sums, f32),
        ],
        in_specs=[HB] * 5,
        out_specs=[VM] * 5,
        scratch_shapes=[gather_room, pltpu.SemaphoreType.DMA((12,))] + pair_room + [stage_room]
        + target_room + list_room,
        compiler_params=PARAMS,
        name="front",
    )(*fixed[:5])
    moved = [lax.ppermute(edge, "bit", [(i, i ^ (1 << n)) for i in range(bits)]) for n in (0, 3, 4, 1, 2)]
    beside = {i: i + 1 for i in range(1, sects - 1, 2)}
    beside.update({j: i for i, j in beside.items()})
    pairs = [
        (b * sects + i, b * sects + beside[i] if i in beside else (b ^ 1) * sects + i)
        for b in range(bits) for i in range(sects)
    ]
    moved.append(lax.ppermute(edge, ("bit", "sect"), pairs))
    moved.append(lax.ppermute(edge, "sect", [(i, i ^ 1) for i in range(sects)]))
    z1, y1, y2, z2, z4, outer, inner = moved
    remote, acc1, centres, table = pl.pallas_call(
        local_kernel,
        out_shape=[
            shape((PAIRS + 8,), i32),
            shape(sums, f32),
            shape((LEAF * 8, PART), f32),
            shape((2 * TABLE, PART), bf16),
        ],
        in_specs=[VM] * 3,
        out_specs=[SM] + [VM] * 3,
        scratch_shapes=[gather_room] + pair_room + [stage_room] + list_room,
        compiler_params=PARAMS,
        name="local_pairs",
    )(near, counts, own)
    return pl.pallas_call(
        remote_kernel,
        out_shape=[shape((3, LEAF, PART), f32)] * 2,
        in_specs=[SM] + [VM] * 5 + [HB] + [VM] * 7,
        out_specs=[VM, VM],
        scratch_shapes=[pltpu.VMEM((12, LEAF), f32), pltpu.SemaphoreType.DMA((1,)), gather_room] + pair_room
        + [list_room[0], pltpu.VMEM(sums, f32)],
        compiler_params=PARAMS,
        name="remote_pairs",
    )(remote, own, centres, table, acc0, acc1, fixed[5], z1, y1, y2, z2, z4, outer, inner)


def solution(mesh):
    in_specs = (
        P(None, ("bit", "sect"), None),
        P(None, ("bit", "sect"), None),
        P(("bit", "sect"), None),
        P(None, ("bit", "sect")),
        P(("bit", "sect"), None),
        P(("bit", "sect")),
    )
    out_specs = (P(None, ("bit", "sect"), None), P(None, ("bit", "sect"), None))
    return jax.shard_map(body, mesh=mesh, in_specs=in_specs, out_specs=out_specs, check_vma=False)
```

```python
import math

import jax
import jax.numpy as jnp
from jax import lax
from jax.experimental import pallas as pl
from jax.experimental.pallas import tpu as pltpu
from jax.sharding import PartitionSpec as P

inv_four_pi = 1.0 / (4.0 * math.pi)
f32, bf16, i32 = jnp.float32, jnp.bfloat16, jnp.int32

LEAF = 32
PART = 128
SLOTS = 8
EDGE = 24
FIELDS = 7
MOVED = FIELDS * EDGE
PAIRS = LEAF * SLOTS
BATCH = 24
HALF = BATCH // 2
ROOM = PAIRS + 2 * BATCH
TABLE = (LEAF + 1) * 32
SUMS = (LEAF + 1) * 16


def rounded(value):
    return value.astype(bf16).astype(f32)


def split3(value):
    high = rounded(value)
    rest = value - high
    mid = rounded(rest)
    return high, mid, rest - mid


def split2(value):
    high = value.astype(bf16)
    return high, (value - high.astype(f32)).astype(bf16)


def leaf_fields(own, group, fields):
    return [own[pl.ds(k * LEAF + group * 8, 8), :] for k in fields]


def offsets(own, group):
    point = leaf_fields(own, group, range(3))
    centre = [jnp.mean(v, axis=1, keepdims=True) for v in point]
    return centre, [v - c for v, c in zip(point, centre)]


def build_targets(own, centres, table, stage):
    for group in range(LEAF // 8):
        centre, off = offsets(own, group)
        a = leaf_fields(own, group, range(3, 6))
        zero = jnp.zeros((8, PART), f32)
        one = jnp.ones((8, PART), f32)
        for k in range(8):
            row = jnp.broadcast_to(centre[k], (8, PART)) if k < 3 else zero
            centres[pl.ds(group * 64 + k, 8, stride=8), :] = row
        left = [split3(-2.0 * v) for v in off]
        right = [split3(-v) for v in a]
        square = split3(off[0] * off[0] + off[1] * off[1] + off[2] * off[2])
        along = split3(off[0] * a[0] + off[1] * a[1] + off[2] * a[2])
        rows = []
        level = [[(left[k][part], right[k][part]) for k in range(3)] for part in range(3)]
        rows += level[0] * 2 + [(one, zero)] * 2
        rows += level[0] + [(one, zero)] + [(square[k], along[k]) for k in range(3)] + [(zero, zero)]
        rows += level[1] * 2 + [(zero, zero)] * 2
        rows += level[2] * 2 + [(zero, zero)] * 2
        for k, (spread_row, proj_row) in enumerate(rows):
            stage[pl.ds(group * 512 + k, 8, stride=32), :] = spread_row
            stage[pl.ds(group * 512 + 256 + k, 8, stride=32), :] = proj_row
        for side in range(2):
            table[pl.ds(side * TABLE + group * 256, 256), :] = stage[
                pl.ds(group * 512 + side * 256, 256), :
            ].astype(bf16)


def source_rows(gathered, left, right, group):
    first = pl.multiple_of(group * 64, 64)
    q = [gathered[pl.ds(first + k, 8, stride=8), :] for k in range(FIELDS)]
    x, a, core = q[:3], q[3:6], q[6]
    part = [split3(v) for v in x]
    size = split3(x[0] * x[0] + x[1] * x[1] + x[2] * x[2] + core * core)
    one = jnp.ones((8, PART), f32)
    rows = [part[k][level] for level in (0, 1) for k in range(3)] + [size[0], size[1]]
    rows += [part[k][2] for k in range(3)] + [size[2]] + [one] * 4
    base = pl.multiple_of(group * 128, 128)
    for k, row in enumerate(rows):
        left[pl.ds(base + k, 8, stride=16), :] = row
    crossed = [
        x[1] * a[2] - x[2] * a[1],
        x[2] * a[0] - x[0] * a[2],
        x[0] * a[1] - x[1] * a[0],
    ]
    for k, row in enumerate(a + crossed):
        high = rounded(row)
        right[pl.ds(base + k, 8, stride=16), :] = high
        right[pl.ds(base + 6 + k, 8, stride=16), :] = row - high


def pair_products(pair, target, table, left):
    rows = left[pl.ds(pl.multiple_of(pair * 16, 16), 16), :]
    lhs = jnp.concatenate([rows, rows[:8], rows[:8]], axis=0).astype(bf16)
    first = pl.multiple_of(target * 32, 32)
    rhs = jnp.concatenate([table[pl.ds(first, 32), :], table[pl.ds(TABLE + first, 32), :]], axis=1)
    return lax.dot_general(lhs, rhs, (((0,), (0,)), ((), ())), preferred_element_type=f32)


def pair_total(pair, both, right):
    spread, proj = both[:, :PART], both[:, PART:]
    root = lax.rsqrt(spread)
    square = root * root
    kernel = root * square
    weight = kernel * square * proj
    k_high, k_low = split2(kernel)
    w_high, w_low = split2(weight)
    pairs = jnp.concatenate(
        [jnp.concatenate([k_high, w_high], axis=1), jnp.concatenate([k_low, w_low], axis=1)], axis=0
    )
    rows = right[pl.ds(pl.multiple_of(pair * 16, 16), 16), :].astype(bf16)
    rows = jnp.concatenate([rows, rows], axis=1)
    return jnp.dot(rows, pairs, preferred_element_type=f32)


def half_batch(begin, now, later, target_of, table, left, right, acc, carry):
    last, total = carry
    results = []
    for lane in range(HALF):
        pair = begin + lane
        if later is not None:
            ahead = pair + HALF
            later[lane] = pair_products(ahead, target_of[ahead], table, left)
        results.append((target_of[pair], pair_total(pair, now[lane], right)))
    for target, value in results:
        total = jnp.where(target == last, total, 0.0) + value
        last = target
        first = pl.multiple_of(target * 16, 16)
        for side in range(2):
            acc[pl.ds(side * SUMS + first, 16), :] = total[:, side * PART : (side + 1) * PART]
    return last, total


def features(count, gathered, left, right):
    def two(step, _):
        source_rows(gathered, left, right, 2 * step)
        source_rows(gathered, left, right, 2 * step + 1)
        return 0

    lax.fori_loop(0, (count + 15) // 16, two, 0)


def sum_pairs(count, target_of, table, left, right, acc, products):
    even, odd = products
    work = (target_of, table, left, right, acc)
    halves = (count + HALF - 1) // HALF

    @pl.when(count > 0)
    def _():
        for lane in range(HALF):
            even[lane] = pair_products(lane, target_of[lane], table, left)

    def step(s, c):
        c = half_batch(s * BATCH, even, odd, *work, c)
        return half_batch(s * BATCH + HALF, odd, even, *work, c)

    carry = (jnp.int32(-1), jnp.zeros((16, 2 * PART), f32))
    carry = lax.fori_loop(0, halves // 2, step, carry)

    @pl.when(halves & 1 == 1)
    def _():
        half_batch((halves - 1) * HALF, even, None, *work, carry)


def slot_codes(near, counts):
    slot = lax.broadcasted_iota(i32, near.shape, 0)
    used = slot < counts
    times = jnp.ones(near.shape, i32)
    fresh = used
    for d in range(1, SLOTS):
        after = pltpu.roll(near, SLOTS - d, 0)
        times = times + ((after == near) & (slot + d < counts)).astype(i32)
        before = pltpu.roll(near, d, 0)
        fresh = fresh & ~((before == near) & (slot >= d))
    owner = near >> 5
    me = jnp.broadcast_to(near[0:1, 0:1] >> 5, near.shape)
    differs = owner ^ me
    bit = differs >> 3
    part = jnp.where(bit == 0, jnp.where(differs == 1, 0, 1), 2)
    for n in range(1, 5):
        part = jnp.where(bit == 1 << n, 2 + n, part)
    mine = differs == 0
    target = lax.broadcasted_iota(i32, near.shape, 1)
    code = jnp.where(mine, 1, 2) + times * 4 + target * 64 + part * 2048 + (near & (LEAF - 1)) * 16384
    return jnp.where(fresh, code, 0)


def early_leaves(codes):
    z = lax.axis_index("bit") & 7
    local = (codes & 1).astype(f32)
    row = lax.broadcasted_iota(i32, (LEAF, LEAF), 0)
    upto = (row <= lax.broadcasted_iota(i32, (LEAF, LEAF), 1)).astype(f32)
    held = jnp.sum(jnp.dot(local, upto, preferred_element_type=f32), axis=0, keepdims=True)
    count = jnp.sum(local).astype(i32)
    ahead = jnp.minimum(count - 8 * (z + 2) - 16, 80)
    leaves = jnp.sum((held <= ahead.astype(f32)).astype(f32)).astype(i32)
    return jnp.where((z < 3) & (ahead >= 12), leaves, 0)


def early_codes(codes, leaves):
    return (codes & 1 == 1) & (lax.broadcasted_iota(i32, codes.shape, 1) < leaves)


def scaled(source, centre, code):
    row = lax.broadcasted_iota(i32, (FIELDS, PART), 0)
    found = source - centre
    return jnp.where((row >= 3) & (row < 6), found * ((code >> 2) & 15).astype(f32), found)


def scan(leaves, codes, own, centres, gathered, targets, remote):
    def leaf(t, carry):
        place, outside = carry
        centre = centres[pl.ds(pl.multiple_of(t * 8, 8), 8), :][:FIELDS]
        for slot in range(SLOTS):
            code = codes[slot, t]
            source = own[pl.ds(code >> 14, FIELDS, stride=LEAF), :]
            gathered[pl.ds(pl.multiple_of(place * 8, 8), FIELDS), :] = scaled(source, centre, code)
            targets[place] = t
            place = place + (code & 1)
            if remote is not None:
                remote[outside] = code
                outside = outside + ((code >> 1) & 1)
        return place, outside

    count, outside = lax.fori_loop(0, leaves, leaf, (jnp.int32(0), jnp.int32(0)))
    if remote is not None:
        for k in range(3):
            remote[outside + k] = 0
        remote[PAIRS + 7] = outside
    close_list(targets, count)
    return count


def close_list(targets, count):
    for lane in range(2 * BATCH):
        targets[count + lane] = LEAF


def fetched(codes, codes_s, sem):
    fetch = pltpu.make_async_copy(codes, codes_s, sem.at[0])
    fetch.start()
    return fetch


def front_kernel(pos, stren, cores, near, counts, own, edge, near_v, counts_v, acc,
                 gathered, sems, left, right, even, odd, stage, centres, table, targets, codes, codes_s, sem):
    copies = []
    for k in range(FIELDS):
        ref, base = ((pos, k), (stren, k - 3), (cores, 0))[min(k // 3, 2)]
        copies.append((ref.at[pl.ds(base * LEAF, EDGE)], edge.at[pl.ds(k * EDGE, EDGE)]))
    copies += [
        (pos, own.at[pl.ds(0, 96)]),
        (stren, own.at[pl.ds(96, 96)]),
        (cores, own.at[pl.ds(192, 32)]),
        (near, near_v),
        (counts, counts_v),
    ]
    copies = [pltpu.make_async_copy(a, b, sems.at[n]) for n, (a, b) in enumerate(copies)]
    for copy in copies:
        copy.start()
    acc[...] = jnp.zeros_like(acc)
    for copy in copies:
        copy.wait()

    @pl.when(lax.axis_index("bit") & 7 < 3)
    def _():
        found = slot_codes(near_v[...], counts_v[...])
        leaves = early_leaves(found)

        @pl.when(leaves > 0)
        def _():
            codes[...] = jnp.where(early_codes(found, leaves), found, 0)
            fetch = fetched(codes, codes_s, sem)
            build_targets(own, centres, table, stage)
            fetch.wait()
            count = scan(leaves, codes_s, own, centres, gathered, targets, None)
            features(count, gathered, left, right)
            sum_pairs(count, targets, table, left, right, acc, (even, odd))


def local_kernel(near, counts, own, remote, acc, centres, table,
                 gathered, left, right, even, odd, stage, targets, codes, codes_s, sem):
    found = slot_codes(near[...], counts[...])
    codes[...] = found

    @pl.when(lax.axis_index("bit") & 7 < 3)
    def _():
        codes[...] = jnp.where(early_codes(found, early_leaves(found)), 0, found)

    fetch = fetched(codes, codes_s, sem)
    build_targets(own, centres, table, stage)
    acc[...] = jnp.zeros_like(acc)
    fetch.wait()
    count = scan(LEAF, codes_s, own, centres, gathered, targets, remote)
    features(count, gathered, left, right)
    sum_pairs(count, targets, table, left, right, acc, (even, odd))


def remote_kernel(remote, own, centres, table, acc0, acc1, far, p1, p8, p16, p2, p4, outer_part, inner_part,
                  velocity, stretching, far_v, sem, gathered, left, right, even, odd, targets, acc):
    parts = (inner_part, outer_part, p1, p2, p4, p8, p16)
    copy = pltpu.make_async_copy(far, far_v, sem.at[0])
    copy.start()
    acc[...] = jnp.zeros_like(acc)
    count = remote[PAIRS + 7]

    def four(step, _):
        for lane in range(4):
            n = step * 4 + lane
            code = remote[n]
            target = (code >> 6) & (LEAF - 1)
            where = pl.ds(code >> 14, FIELDS, stride=EDGE)
            part = (code >> 11) & 7
            source = parts[0][where, :]
            for k in range(1, 7):
                source = jnp.where(part == k, parts[k][where, :], source)
            centre = centres[pl.ds(pl.multiple_of(target * 8, 8), 8), :][:FIELDS]
            gathered[pl.ds(pl.multiple_of(n * 8, 8), FIELDS), :] = scaled(source, centre, code)
            targets[n] = target
        return 0

    lax.fori_loop(0, (count + 3) // 4, four, 0)
    close_list(targets, count)
    features(count, gathered, left, right)
    sum_pairs(count, targets, table, left, right, acc, (even, odd))
    copy.wait()

    coefs = far_v[...].T
    for group in range(LEAF // 8):
        rows = pl.ds(group * 8, 8)
        _, off = offsets(own, group)
        a = leaf_fields(own, group, range(3, 6))

        def summed(field, side):
            first = side * SUMS + group * 128 + field
            parts = [
                ref[pl.ds(first + low, 8, stride=16), :] for ref in (acc0, acc1, acc) for low in (0, 6)
            ]
            return (parts[0] + parts[1]) + (parts[2] + parts[3]) + (parts[4] + parts[5])

        ka = [summed(k, 0) for k in range(3)]
        kc = [summed(3 + k, 0) for k in range(3)]
        wa = [summed(k, 1) for k in range(3)]
        wc = [summed(3 + k, 1) for k in range(3)]
        coef = [coefs[group * 8 : group * 8 + 8, k : k + 1] for k in range(12)]
        for i in range(3):
            j, k = (i + 1) % 3, (i + 2) % 3
            near_vel = off[j] * ka[k] - off[k] * ka[j] - kc[i]
            steep = off[j] * wa[k] - off[k] * wa[j] - wc[i]
            near_str = a[j] * ka[k] - a[k] * ka[j] - 3.0 * steep
            grad = [coef[3 + 3 * i + m] for m in range(3)]
            velocity[i, rows, :] = (
                -inv_four_pi * near_vel + coef[i]
                + grad[0] * off[0] + grad[1] * off[1] + grad[2] * off[2]
            )
            stretching[i, rows, :] = (
                -inv_four_pi * near_str + grad[0] * a[0] + grad[1] * a[1] + grad[2] * a[2]
            )


VM = pl.BlockSpec(memory_space=pltpu.VMEM)
SM = pl.BlockSpec(memory_space=pltpu.SMEM)
HB = pl.BlockSpec(memory_space=pltpu.HBM)
PARAMS = pltpu.CompilerParams(vmem_limit_bytes=24 * 2**20)


def body(positions, strengths, cores, far_coef, near_list, near_count):
    bits, sects = lax.axis_size("bit"), lax.axis_size("sect")
    shape = jax.ShapeDtypeStruct
    source_room = [pltpu.VMEM((ROOM * 16, PART), f32), pltpu.VMEM((ROOM * 16, PART), f32)]
    pair_room = source_room + [pltpu.VMEM((HALF, PART, 2 * PART), f32)] * 2
    stage_room = pltpu.VMEM((2048, PART), f32)
    target_room = [pltpu.VMEM((LEAF * 8, PART), f32), pltpu.VMEM((2 * TABLE, PART), bf16)]
    list_room = [
        pltpu.SMEM((ROOM,), i32),
        pltpu.VMEM((SLOTS, LEAF), i32),
        pltpu.SMEM((SLOTS, LEAF), i32),
        pltpu.SemaphoreType.DMA((1,)),
    ]
    gather_room = pltpu.VMEM((ROOM * 8, PART), f32)
    sums = (2 * SUMS, PART)
    fixed = [
        pltpu.with_memory_space_constraint(v, pltpu.HBM)
        for v in (
            positions.reshape(3 * LEAF, PART),
            strengths.reshape(3 * LEAF, PART),
            cores,
            near_list.T,
            near_count.reshape(1, LEAF),
            far_coef,
        )
    ]
    own, edge, near, counts, acc0 = pl.pallas_call(
        front_kernel,
        out_shape=[
            shape((LEAF * FIELDS, PART), f32),
            shape((MOVED, PART), f32),
            shape((SLOTS, LEAF), i32),
            shape((1, LEAF), i32),
            shape(sums, f32),
        ],
        in_specs=[HB] * 5,
        out_specs=[VM] * 5,
        scratch_shapes=[gather_room, pltpu.SemaphoreType.DMA((12,))] + pair_room + [stage_room]
        + target_room + list_room,
        compiler_params=PARAMS,
        name="front",
    )(*fixed[:5])
    moved = [lax.ppermute(edge, "bit", [(i, i ^ (1 << n)) for i in range(bits)]) for n in (0, 3, 4, 1, 2)]
    beside = {i: i + 1 for i in range(1, sects - 1, 2)}
    beside.update({j: i for i, j in beside.items()})
    pairs = [
        (b * sects + i, b * sects + beside[i] if i in beside else (b ^ 1) * sects + i)
        for b in range(bits) for i in range(sects)
    ]
    moved.append(lax.ppermute(edge, ("bit", "sect"), pairs))
    moved.append(lax.ppermute(edge, "sect", [(i, i ^ 1) for i in range(sects)]))
    z1, y1, y2, z2, z4, outer, inner = moved
    remote, acc1, centres, table = pl.pallas_call(
        local_kernel,
        out_shape=[
            shape((PAIRS + 8,), i32),
            shape(sums, f32),
            shape((LEAF * 8, PART), f32),
            shape((2 * TABLE, PART), bf16),
        ],
        in_specs=[VM] * 3,
        out_specs=[SM] + [VM] * 3,
        scratch_shapes=[gather_room] + pair_room + [stage_room] + list_room,
        compiler_params=PARAMS,
        name="local_pairs",
    )(near, counts, own)
    return pl.pallas_call(
        remote_kernel,
        out_shape=[shape((3, LEAF, PART), f32)] * 2,
        in_specs=[SM] + [VM] * 5 + [HB] + [VM] * 7,
        out_specs=[VM, VM],
        scratch_shapes=[pltpu.VMEM((12, LEAF), f32), pltpu.SemaphoreType.DMA((1,)), gather_room] + pair_room
        + [list_room[0], pltpu.VMEM(sums, f32)],
        compiler_params=PARAMS,
        name="remote_pairs",
    )(remote, own, centres, table, acc0, acc1, fixed[5], z1, y1, y2, z2, z4, outer, inner)


def solution(mesh):
    in_specs = (
        P(None, ("bit", "sect"), None),
        P(None, ("bit", "sect"), None),
        P(("bit", "sect"), None),
        P(None, ("bit", "sect")),
        P(("bit", "sect"), None),
        P(("bit", "sect")),
    )
    out_specs = (P(None, ("bit", "sect"), None), P(None, ("bit", "sect"), None))
    return jax.shard_map(body, mesh=mesh, in_specs=in_specs, out_specs=out_specs, check_vma=False)
```

```python
import math

import jax
import jax.numpy as jnp
from jax import lax
from jax.experimental import pallas as pl
from jax.experimental.pallas import tpu as pltpu
from jax.sharding import PartitionSpec as P

inv_four_pi = 1.0 / (4.0 * math.pi)
f32, bf16, i32 = jnp.float32, jnp.bfloat16, jnp.int32

LEAF = 32
PART = 128
SLOTS = 8
EDGE = 24
FIELDS = 7
MOVED = FIELDS * EDGE
PAIRS = LEAF * SLOTS
BATCH = 24
HALF = BATCH // 2
ROOM = PAIRS + 2 * BATCH
TABLE = (LEAF + 1) * 32
SUMS = (LEAF + 1) * 16


def rounded(value):
    return value.astype(bf16).astype(f32)


def split3(value):
    high = rounded(value)
    rest = value - high
    mid = rounded(rest)
    return high, mid, rest - mid


def split2(value):
    high = value.astype(bf16)
    return high, (value - high.astype(f32)).astype(bf16)


def leaf_fields(own, group, fields):
    return [own[pl.ds(k * LEAF + group * 8, 8), :] for k in fields]


def offsets(own, group):
    point = leaf_fields(own, group, range(3))
    centre = [jnp.mean(v, axis=1, keepdims=True) for v in point]
    return centre, [v - c for v, c in zip(point, centre)]


def build_targets(own, centres, table, stage):
    for group in range(LEAF // 8):
        centre, off = offsets(own, group)
        a = leaf_fields(own, group, range(3, 6))
        zero = jnp.zeros((8, PART), f32)
        one = jnp.ones((8, PART), f32)
        for k in range(8):
            row = jnp.broadcast_to(centre[k], (8, PART)) if k < 3 else zero
            centres[pl.ds(group * 64 + k, 8, stride=8), :] = row
        left = [split3(-2.0 * v) for v in off]
        right = [split3(-v) for v in a]
        square = split3(off[0] * off[0] + off[1] * off[1] + off[2] * off[2])
        along = split3(off[0] * a[0] + off[1] * a[1] + off[2] * a[2])
        rows = []
        level = [[(left[k][part], right[k][part]) for k in range(3)] for part in range(3)]
        rows += level[0] * 2 + [(one, zero)] * 2
        rows += level[0] + [(one, zero)] + [(square[k], along[k]) for k in range(3)] + [(zero, zero)]
        rows += level[1] * 2 + [(zero, zero)] * 2
        rows += level[2] * 2 + [(zero, zero)] * 2
        for k, (spread_row, proj_row) in enumerate(rows):
            stage[pl.ds(group * 512 + k, 8, stride=32), :] = spread_row
            stage[pl.ds(group * 512 + 256 + k, 8, stride=32), :] = proj_row
        for side in range(2):
            table[pl.ds(side * TABLE + group * 256, 256), :] = stage[
                pl.ds(group * 512 + side * 256, 256), :
            ].astype(bf16)


def source_fields(gathered, group):
    first = pl.multiple_of(group * 64, 64)
    return [gathered[pl.ds(first + k, 8, stride=8), :] for k in range(FIELDS)]


def source_rows(q, left, right, group):
    x, a, core = q[:3], q[3:6], q[6]
    part = [split3(v) for v in x]
    size = split3(x[0] * x[0] + x[1] * x[1] + x[2] * x[2] + core * core)
    one = jnp.ones((8, PART), f32)
    rows = [part[k][level] for level in (0, 1) for k in range(3)] + [size[0], size[1]]
    rows += [part[k][2] for k in range(3)] + [size[2]] + [one] * 4
    base = pl.multiple_of(group * 128, 128)
    for k, row in enumerate(rows):
        left[pl.ds(base + k, 8, stride=16), :] = row
    crossed = [
        x[1] * a[2] - x[2] * a[1],
        x[2] * a[0] - x[0] * a[2],
        x[0] * a[1] - x[1] * a[0],
    ]
    for k, row in enumerate(a + crossed):
        high = rounded(row)
        right[pl.ds(base + k, 8, stride=16), :] = high
        right[pl.ds(base + 6 + k, 8, stride=16), :] = row - high


def pair_products(pair, target, table, left):
    rows = left[pl.ds(pl.multiple_of(pair * 16, 16), 16), :]
    lhs = jnp.concatenate([rows, rows[:8], rows[:8]], axis=0).astype(bf16)
    first = pl.multiple_of(target * 32, 32)
    rhs = jnp.concatenate([table[pl.ds(first, 32), :], table[pl.ds(TABLE + first, 32), :]], axis=1)
    return lax.dot_general(lhs, rhs, (((0,), (0,)), ((), ())), preferred_element_type=f32)


def pair_total(pair, both, right):
    spread, proj = both[:, :PART], both[:, PART:]
    root = lax.rsqrt(spread)
    square = root * root
    kernel = root * square
    weight = kernel * square * proj
    k_high, k_low = split2(kernel)
    w_high, w_low = split2(weight)
    pairs = jnp.concatenate(
        [jnp.concatenate([k_high, w_high], axis=1), jnp.concatenate([k_low, w_low], axis=1)], axis=0
    )
    rows = right[pl.ds(pl.multiple_of(pair * 16, 16), 16), :].astype(bf16)
    rows = jnp.concatenate([rows, rows], axis=1)
    return jnp.dot(rows, pairs, preferred_element_type=f32)


def half_batch(begin, now, later, target_of, table, left, right, acc, carry):
    last, total = carry
    results = []
    for lane in range(HALF):
        pair = begin + lane
        if later is not None:
            ahead = pair + HALF
            later[lane] = pair_products(ahead, target_of[ahead], table, left)
        results.append((target_of[pair], pair_total(pair, now[lane], right)))
    for target, value in results:
        total = jnp.where(target == last, total, 0.0) + value
        last = target
        first = pl.multiple_of(target * 16, 16)
        for side in range(2):
            acc[pl.ds(side * SUMS + first, 16), :] = total[:, side * PART : (side + 1) * PART]
    return last, total


def features(count, gathered, left, right):
    def two(step, _):
        groups = (2 * step, 2 * step + 1)
        for group, fields in [(g, source_fields(gathered, g)) for g in groups]:
            source_rows(fields, left, right, group)
        return 0

    lax.fori_loop(0, (count + 15) // 16, two, 0)


def sum_pairs(count, target_of, table, left, right, acc, products):
    even, odd = products
    work = (target_of, table, left, right, acc)
    halves = (count + HALF - 1) // HALF

    @pl.when(count > 0)
    def _():
        for lane in range(HALF):
            even[lane] = pair_products(lane, target_of[lane], table, left)

    def step(s, c):
        c = half_batch(s * BATCH, even, odd, *work, c)
        return half_batch(s * BATCH + HALF, odd, even, *work, c)

    carry = (jnp.int32(-1), jnp.zeros((16, 2 * PART), f32))
    carry = lax.fori_loop(0, halves // 2, step, carry)

    @pl.when(halves & 1 == 1)
    def _():
        half_batch((halves - 1) * HALF, even, None, *work, carry)


def slot_codes(near, counts):
    slot = lax.broadcasted_iota(i32, near.shape, 0)
    used = slot < counts
    times = jnp.ones(near.shape, i32)
    fresh = used
    for d in range(1, SLOTS):
        after = pltpu.roll(near, SLOTS - d, 0)
        times = times + ((after == near) & (slot + d < counts)).astype(i32)
        before = pltpu.roll(near, d, 0)
        fresh = fresh & ~((before == near) & (slot >= d))
    owner = near >> 5
    me = jnp.broadcast_to(near[0:1, 0:1] >> 5, near.shape)
    differs = owner ^ me
    bit = differs >> 3
    part = jnp.where(bit == 0, jnp.where(differs == 1, 0, 1), 2)
    for n in range(1, 5):
        part = jnp.where(bit == 1 << n, 2 + n, part)
    mine = differs == 0
    target = lax.broadcasted_iota(i32, near.shape, 1)
    code = jnp.where(mine, 1, 2) + times * 4 + target * 64 + part * 2048 + (near & (LEAF - 1)) * 16384
    return jnp.where(fresh, code, 0)


def early_leaves(codes):
    z = lax.axis_index("bit") & 7
    local = (codes & 1).astype(f32)
    row = lax.broadcasted_iota(i32, (LEAF, LEAF), 0)
    upto = (row <= lax.broadcasted_iota(i32, (LEAF, LEAF), 1)).astype(f32)
    held = jnp.sum(jnp.dot(local, upto, preferred_element_type=f32), axis=0, keepdims=True)
    count = jnp.sum(local).astype(i32)
    ahead = jnp.minimum(count - 8 * (z + 2) - 16, 80)
    leaves = jnp.sum((held <= ahead.astype(f32)).astype(f32)).astype(i32)
    return jnp.where((z < 3) & (ahead >= 12), leaves, 0)


def early_codes(codes, leaves):
    return (codes & 1 == 1) & (lax.broadcasted_iota(i32, codes.shape, 1) < leaves)


def scaled(source, centre, code):
    row = lax.broadcasted_iota(i32, (FIELDS, PART), 0)
    found = source - centre
    return jnp.where((row >= 3) & (row < 6), found * ((code >> 2) & 15).astype(f32), found)


def scan(leaves, codes, own, centres, gathered, targets, remote):
    def leaf(t, carry):
        place, outside = carry
        centre = centres[pl.ds(pl.multiple_of(t * 8, 8), 8), :][:FIELDS]
        listed = [codes[slot, t] for slot in range(SLOTS)]
        sources = [
            scaled(own[pl.ds(code >> 14, FIELDS, stride=LEAF), :], centre, code) for code in listed
        ]
        for code, source in zip(listed, sources):
            gathered[pl.ds(pl.multiple_of(place * 8, 8), FIELDS), :] = source
            targets[place] = t
            place = place + (code & 1)
            if remote is not None:
                remote[outside] = code
                outside = outside + ((code >> 1) & 1)
        return place, outside

    count, outside = lax.fori_loop(0, leaves, leaf, (jnp.int32(0), jnp.int32(0)))
    if remote is not None:
        for k in range(3):
            remote[outside + k] = 0
        remote[PAIRS + 7] = outside
    close_list(targets, count)
    return count


def close_list(targets, count):
    for lane in range(2 * BATCH):
        targets[count + lane] = LEAF


def fetched(codes, codes_s, sem):
    fetch = pltpu.make_async_copy(codes, codes_s, sem.at[0])
    fetch.start()
    return fetch


def front_kernel(pos, stren, cores, near, counts, own, edge, near_v, counts_v, acc,
                 gathered, sems, left, right, even, odd, stage, centres, table, targets, codes, codes_s, sem):
    copies = []
    for k in range(FIELDS):
        ref, base = ((pos, k), (stren, k - 3), (cores, 0))[min(k // 3, 2)]
        copies.append((ref.at[pl.ds(base * LEAF, EDGE)], edge.at[pl.ds(k * EDGE, EDGE)]))
    copies += [
        (pos, own.at[pl.ds(0, 96)]),
        (stren, own.at[pl.ds(96, 96)]),
        (cores, own.at[pl.ds(192, 32)]),
        (near, near_v),
        (counts, counts_v),
    ]
    copies = [pltpu.make_async_copy(a, b, sems.at[n]) for n, (a, b) in enumerate(copies)]
    for copy in copies:
        copy.start()
    acc[...] = jnp.zeros_like(acc)
    for copy in copies:
        copy.wait()

    @pl.when(lax.axis_index("bit") & 7 < 3)
    def _():
        found = slot_codes(near_v[...], counts_v[...])
        leaves = early_leaves(found)

        @pl.when(leaves > 0)
        def _():
            codes[...] = jnp.where(early_codes(found, leaves), found, 0)
            fetch = fetched(codes, codes_s, sem)
            build_targets(own, centres, table, stage)
            fetch.wait()
            count = scan(leaves, codes_s, own, centres, gathered, targets, None)
            features(count, gathered, left, right)
            sum_pairs(count, targets, table, left, right, acc, (even, odd))


def local_kernel(near, counts, own, remote, acc, centres, table,
                 gathered, left, right, even, odd, stage, targets, codes, codes_s, sem):
    found = slot_codes(near[...], counts[...])
    codes[...] = found

    @pl.when(lax.axis_index("bit") & 7 < 3)
    def _():
        codes[...] = jnp.where(early_codes(found, early_leaves(found)), 0, found)

    fetch = fetched(codes, codes_s, sem)
    build_targets(own, centres, table, stage)
    acc[...] = jnp.zeros_like(acc)
    fetch.wait()
    count = scan(LEAF, codes_s, own, centres, gathered, targets, remote)
    features(count, gathered, left, right)
    sum_pairs(count, targets, table, left, right, acc, (even, odd))


def remote_kernel(remote, own, centres, table, acc0, acc1, far, p1, p8, p16, p2, p4, outer_part, inner_part,
                  velocity, stretching, far_v, sem, gathered, left, right, even, odd, targets, acc):
    parts = (inner_part, outer_part, p1, p2, p4, p8, p16)
    copy = pltpu.make_async_copy(far, far_v, sem.at[0])
    copy.start()
    acc[...] = jnp.zeros_like(acc)
    count = remote[PAIRS + 7]

    def four(step, _):
        found = []
        for code in [remote[step * 4 + lane] for lane in range(4)]:
            target = (code >> 6) & (LEAF - 1)
            where = pl.ds(code >> 14, FIELDS, stride=EDGE)
            part = (code >> 11) & 7
            source = parts[0][where, :]
            for k in range(1, 7):
                source = jnp.where(part == k, parts[k][where, :], source)
            centre = centres[pl.ds(pl.multiple_of(target * 8, 8), 8), :][:FIELDS]
            found.append((target, scaled(source, centre, code)))
        for lane, (target, source) in enumerate(found):
            n = step * 4 + lane
            gathered[pl.ds(pl.multiple_of(n * 8, 8), FIELDS), :] = source
            targets[n] = target
        return 0

    lax.fori_loop(0, (count + 3) // 4, four, 0)
    close_list(targets, count)
    features(count, gathered, left, right)
    sum_pairs(count, targets, table, left, right, acc, (even, odd))
    copy.wait()

    coefs = far_v[...].T
    for group in range(LEAF // 8):
        rows = pl.ds(group * 8, 8)
        _, off = offsets(own, group)
        a = leaf_fields(own, group, range(3, 6))

        def summed(field, side):
            first = side * SUMS + group * 128 + field
            parts = [
                ref[pl.ds(first + low, 8, stride=16), :] for ref in (acc0, acc1, acc) for low in (0, 6)
            ]
            return (parts[0] + parts[1]) + (parts[2] + parts[3]) + (parts[4] + parts[5])

        ka = [summed(k, 0) for k in range(3)]
        kc = [summed(3 + k, 0) for k in range(3)]
        wa = [summed(k, 1) for k in range(3)]
        wc = [summed(3 + k, 1) for k in range(3)]
        coef = [coefs[group * 8 : group * 8 + 8, k : k + 1] for k in range(12)]
        for i in range(3):
            j, k = (i + 1) % 3, (i + 2) % 3
            near_vel = off[j] * ka[k] - off[k] * ka[j] - kc[i]
            steep = off[j] * wa[k] - off[k] * wa[j] - wc[i]
            near_str = a[j] * ka[k] - a[k] * ka[j] - 3.0 * steep
            grad = [coef[3 + 3 * i + m] for m in range(3)]
            velocity[i, rows, :] = (
                -inv_four_pi * near_vel + coef[i]
                + grad[0] * off[0] + grad[1] * off[1] + grad[2] * off[2]
            )
            stretching[i, rows, :] = (
                -inv_four_pi * near_str + grad[0] * a[0] + grad[1] * a[1] + grad[2] * a[2]
            )


VM = pl.BlockSpec(memory_space=pltpu.VMEM)
SM = pl.BlockSpec(memory_space=pltpu.SMEM)
HB = pl.BlockSpec(memory_space=pltpu.HBM)
PARAMS = pltpu.CompilerParams(vmem_limit_bytes=24 * 2**20)


def body(positions, strengths, cores, far_coef, near_list, near_count):
    bits, sects = lax.axis_size("bit"), lax.axis_size("sect")
    shape = jax.ShapeDtypeStruct
    source_room = [pltpu.VMEM((ROOM * 16, PART), f32), pltpu.VMEM((ROOM * 16, PART), f32)]
    pair_room = source_room + [pltpu.VMEM((HALF, PART, 2 * PART), f32)] * 2
    stage_room = pltpu.VMEM((2048, PART), f32)
    target_room = [pltpu.VMEM((LEAF * 8, PART), f32), pltpu.VMEM((2 * TABLE, PART), bf16)]
    list_room = [
        pltpu.SMEM((ROOM,), i32),
        pltpu.VMEM((SLOTS, LEAF), i32),
        pltpu.SMEM((SLOTS, LEAF), i32),
        pltpu.SemaphoreType.DMA((1,)),
    ]
    gather_room = pltpu.VMEM((ROOM * 8, PART), f32)
    sums = (2 * SUMS, PART)
    fixed = [
        pltpu.with_memory_space_constraint(v, pltpu.HBM)
        for v in (
            positions.reshape(3 * LEAF, PART),
            strengths.reshape(3 * LEAF, PART),
            cores,
            near_list.T,
            near_count.reshape(1, LEAF),
            far_coef,
        )
    ]
    own, edge, near, counts, acc0 = pl.pallas_call(
        front_kernel,
        out_shape=[
            shape((LEAF * FIELDS, PART), f32),
            shape((MOVED, PART), f32),
            shape((SLOTS, LEAF), i32),
            shape((1, LEAF), i32),
            shape(sums, f32),
        ],
        in_specs=[HB] * 5,
        out_specs=[VM] * 5,
        scratch_shapes=[gather_room, pltpu.SemaphoreType.DMA((12,))] + pair_room + [stage_room]
        + target_room + list_room,
        compiler_params=PARAMS,
        name="front",
    )(*fixed[:5])
    moved = [lax.ppermute(edge, "bit", [(i, i ^ (1 << n)) for i in range(bits)]) for n in (0, 3, 4, 1, 2)]
    beside = {i: i + 1 for i in range(1, sects - 1, 2)}
    beside.update({j: i for i, j in beside.items()})
    pairs = [
        (b * sects + i, b * sects + beside[i] if i in beside else (b ^ 1) * sects + i)
        for b in range(bits) for i in range(sects)
    ]
    moved.append(lax.ppermute(edge, ("bit", "sect"), pairs))
    moved.append(lax.ppermute(edge, "sect", [(i, i ^ 1) for i in range(sects)]))
    z1, y1, y2, z2, z4, outer, inner = moved
    remote, acc1, centres, table = pl.pallas_call(
        local_kernel,
        out_shape=[
            shape((PAIRS + 8,), i32),
            shape(sums, f32),
            shape((LEAF * 8, PART), f32),
            shape((2 * TABLE, PART), bf16),
        ],
        in_specs=[VM] * 3,
        out_specs=[SM] + [VM] * 3,
        scratch_shapes=[gather_room] + pair_room + [stage_room] + list_room,
        compiler_params=PARAMS,
        name="local_pairs",
    )(near, counts, own)
    return pl.pallas_call(
        remote_kernel,
        out_shape=[shape((3, LEAF, PART), f32)] * 2,
        in_specs=[SM] + [VM] * 5 + [HB] + [VM] * 7,
        out_specs=[VM, VM],
        scratch_shapes=[pltpu.VMEM((12, LEAF), f32), pltpu.SemaphoreType.DMA((1,)), gather_room] + pair_room
        + [list_room[0], pltpu.VMEM(sums, f32)],
        compiler_params=PARAMS,
        name="remote_pairs",
    )(remote, own, centres, table, acc0, acc1, fixed[5], z1, y1, y2, z2, z4, outer, inner)


def solution(mesh):
    in_specs = (
        P(None, ("bit", "sect"), None),
        P(None, ("bit", "sect"), None),
        P(("bit", "sect"), None),
        P(None, ("bit", "sect")),
        P(("bit", "sect"), None),
        P(("bit", "sect")),
    )
    out_specs = (P(None, ("bit", "sect"), None), P(None, ("bit", "sect"), None))
    return jax.shard_map(body, mesh=mesh, in_specs=in_specs, out_specs=out_specs, check_vma=False)
```

```python
import math

import jax
import jax.numpy as jnp
from jax import lax
from jax.experimental import pallas as pl
from jax.experimental.pallas import tpu as pltpu
from jax.sharding import PartitionSpec as P

inv_four_pi = 1.0 / (4.0 * math.pi)
f32, bf16, i32 = jnp.float32, jnp.bfloat16, jnp.int32

LEAF = 32
PART = 128
SLOTS = 8
EDGE = 24
FIELDS = 7
MOVED = FIELDS * EDGE
PAIRS = LEAF * SLOTS
BATCH = 24
HALF = BATCH // 2
ROOM = PAIRS + 2 * BATCH
TABLE = (LEAF + 1) * 32
SUMS = (LEAF + 1) * 16


def rounded(value):
    return value.astype(bf16).astype(f32)


def split3(value):
    high = rounded(value)
    rest = value - high
    mid = rounded(rest)
    return high, mid, rest - mid


def split2(value):
    high = value.astype(bf16)
    return high, (value - high.astype(f32)).astype(bf16)


def leaf_fields(own, group, fields):
    return [own[pl.ds(k * LEAF + group * 8, 8), :] for k in fields]


def offsets(own, group):
    point = leaf_fields(own, group, range(3))
    centre = [jnp.mean(v, axis=1, keepdims=True) for v in point]
    return centre, [v - c for v, c in zip(point, centre)]


def build_targets(own, centres, table, stage):
    for group in range(LEAF // 8):
        centre, off = offsets(own, group)
        a = leaf_fields(own, group, range(3, 6))
        zero = jnp.zeros((8, PART), f32)
        one = jnp.ones((8, PART), f32)
        for k in range(8):
            row = jnp.broadcast_to(centre[k], (8, PART)) if k < 3 else zero
            centres[pl.ds(group * 64 + k, 8, stride=8), :] = row
        left = [split3(-2.0 * v) for v in off]
        right = [split3(-v) for v in a]
        square = split3(off[0] * off[0] + off[1] * off[1] + off[2] * off[2])
        along = split3(off[0] * a[0] + off[1] * a[1] + off[2] * a[2])
        rows = []
        level = [[(left[k][part], right[k][part]) for k in range(3)] for part in range(3)]
        rows += level[0] * 2 + [(one, zero)] * 2
        rows += level[0] + [(one, zero)] + [(square[k], along[k]) for k in range(3)] + [(zero, zero)]
        rows += level[1] * 2 + [(zero, zero)] * 2
        rows += level[2] * 2 + [(zero, zero)] * 2
        for k, (spread_row, proj_row) in enumerate(rows):
            stage[pl.ds(group * 512 + k, 8, stride=32), :] = spread_row
            stage[pl.ds(group * 512 + 256 + k, 8, stride=32), :] = proj_row
        for side in range(2):
            table[pl.ds(side * TABLE + group * 256, 256), :] = stage[
                pl.ds(group * 512 + side * 256, 256), :
            ].astype(bf16)


def source_fields(gathered, group):
    first = pl.multiple_of(group * 64, 64)
    return [gathered[pl.ds(first + k, 8, stride=8), :] for k in range(FIELDS)]


def source_rows(q, left, right, group):
    x, a, core = q[:3], q[3:6], q[6]
    part = [split3(v) for v in x]
    size = split3(x[0] * x[0] + x[1] * x[1] + x[2] * x[2] + core * core)
    one = jnp.ones((8, PART), f32)
    rows = [part[k][level] for level in (0, 1) for k in range(3)] + [size[0], size[1]]
    rows += [part[k][2] for k in range(3)] + [size[2]] + [one] * 4
    base = pl.multiple_of(group * 128, 128)
    for k, row in enumerate(rows):
        left[pl.ds(base + k, 8, stride=16), :] = row
    crossed = [
        x[1] * a[2] - x[2] * a[1],
        x[2] * a[0] - x[0] * a[2],
        x[0] * a[1] - x[1] * a[0],
    ]
    for k, row in enumerate(a + crossed):
        high = rounded(row)
        right[pl.ds(base + k, 8, stride=16), :] = high
        right[pl.ds(base + 6 + k, 8, stride=16), :] = row - high


def pair_products(pair, target, table, left):
    rows = left[pl.ds(pl.multiple_of(pair * 16, 16), 16), :]
    lhs = jnp.concatenate([rows, rows[:8], rows[:8]], axis=0).astype(bf16)
    first = pl.multiple_of(target * 32, 32)
    rhs = jnp.concatenate([table[pl.ds(first, 32), :], table[pl.ds(TABLE + first, 32), :]], axis=1)
    return lax.dot_general(lhs, rhs, (((0,), (0,)), ((), ())), preferred_element_type=f32)


def pair_total(pair, both, right):
    spread, proj = both[:, :PART], both[:, PART:]
    root = lax.rsqrt(spread)
    square = root * root
    kernel = root * square
    weight = kernel * square * proj
    k_high, k_low = split2(kernel)
    w_high, w_low = split2(weight)
    pairs = jnp.concatenate(
        [jnp.concatenate([k_high, w_high], axis=1), jnp.concatenate([k_low, w_low], axis=1)], axis=0
    )
    rows = right[pl.ds(pl.multiple_of(pair * 16, 16), 16), :].astype(bf16)
    rows = jnp.concatenate([rows, rows], axis=1)
    return jnp.dot(rows, pairs, preferred_element_type=f32)


def half_batch(begin, now, later, target_of, table, left, right, acc, carry):
    last, total = carry
    results = []
    for lane in range(HALF):
        pair = begin + lane
        if later is not None:
            ahead = pair + HALF
            later[lane] = pair_products(ahead, target_of[ahead], table, left)
        results.append((target_of[pair], pair_total(pair, now[lane], right)))
    for target, value in results:
        total = jnp.where(target == last, total, 0.0) + value
        last = target
        first = pl.multiple_of(target * 16, 16)
        for side in range(2):
            acc[pl.ds(side * SUMS + first, 16), :] = total[:, side * PART : (side + 1) * PART]
    return last, total


def features(count, gathered, left, right):
    def two(step, _):
        groups = (2 * step, 2 * step + 1)
        for group, fields in [(g, source_fields(gathered, g)) for g in groups]:
            source_rows(fields, left, right, group)
        return 0

    lax.fori_loop(0, (count + 15) // 16, two, 0)


def sum_pairs(count, target_of, table, left, right, acc, products):
    even, odd = products
    work = (target_of, table, left, right, acc)
    halves = (count + HALF - 1) // HALF

    @pl.when(count > 0)
    def _():
        for lane in range(HALF):
            even[lane] = pair_products(lane, target_of[lane], table, left)

    def step(s, c):
        c = half_batch(s * BATCH, even, odd, *work, c)
        return half_batch(s * BATCH + HALF, odd, even, *work, c)

    carry = (jnp.int32(-1), jnp.zeros((16, 2 * PART), f32))
    carry = lax.fori_loop(0, halves // 2, step, carry)

    @pl.when(halves & 1 == 1)
    def _():
        half_batch((halves - 1) * HALF, even, None, *work, carry)


def slot_codes(near, counts):
    slot = lax.broadcasted_iota(i32, near.shape, 0)
    used = slot < counts
    times = jnp.ones(near.shape, i32)
    fresh = used
    for d in range(1, SLOTS):
        after = pltpu.roll(near, SLOTS - d, 0)
        times = times + ((after == near) & (slot + d < counts)).astype(i32)
        before = pltpu.roll(near, d, 0)
        fresh = fresh & ~((before == near) & (slot >= d))
    owner = near >> 5
    me = jnp.broadcast_to(near[0:1, 0:1] >> 5, near.shape)
    differs = owner ^ me
    bit = differs >> 3
    part = jnp.where(bit == 0, jnp.where(differs == 1, 0, 1), 2)
    for n in range(1, 5):
        part = jnp.where(bit == 1 << n, 2 + n, part)
    mine = differs == 0
    target = lax.broadcasted_iota(i32, near.shape, 1)
    code = jnp.where(mine, 1, 2) + times * 4 + target * 64 + part * 2048 + (near & (LEAF - 1)) * 16384
    return jnp.where(fresh, code, 0)


def early_leaves(codes):
    z = lax.axis_index("bit") & 7
    local = (codes & 1).astype(f32)
    row = lax.broadcasted_iota(i32, (LEAF, LEAF), 0)
    upto = (row <= lax.broadcasted_iota(i32, (LEAF, LEAF), 1)).astype(f32)
    held = jnp.sum(jnp.dot(local, upto, preferred_element_type=f32), axis=0, keepdims=True)
    count = jnp.sum(local).astype(i32)
    ahead = jnp.minimum(count - 8 * (z + 2) - 16, 80)
    leaves = jnp.sum((held <= ahead.astype(f32)).astype(f32)).astype(i32)
    return jnp.where((z < 3) & (ahead >= 12), leaves, 0)


def early_codes(codes, leaves):
    return (codes & 1 == 1) & (lax.broadcasted_iota(i32, codes.shape, 1) < leaves)


def scaled(source, centre, code):
    row = lax.broadcasted_iota(i32, (FIELDS, PART), 0)
    found = source - centre
    return jnp.where((row >= 3) & (row < 6), found * ((code >> 2) & 15).astype(f32), found)


def scan(leaves, codes, own, centres, gathered, targets, remote):
    def leaf(t, carry):
        place, outside = carry
        centre = centres[pl.ds(pl.multiple_of(t * 8, 8), 8), :][:FIELDS]
        listed = [codes[slot, t] for slot in range(SLOTS)]
        sources = [
            scaled(own[pl.ds(code >> 14, FIELDS, stride=LEAF), :], centre, code) for code in listed
        ]
        for code, source in zip(listed, sources):
            gathered[pl.ds(pl.multiple_of(place * 8, 8), FIELDS), :] = source
            targets[place] = t
            place = place + (code & 1)
            if remote is not None:
                remote[outside] = code
                outside = outside + ((code >> 1) & 1)
        return place, outside

    count, outside = lax.fori_loop(0, leaves, leaf, (jnp.int32(0), jnp.int32(0)))
    if remote is not None:
        for k in range(3):
            remote[outside + k] = 0
        remote[PAIRS + 7] = outside
    close_list(targets, count)
    return count


def close_list(targets, count):
    for lane in range(2 * BATCH):
        targets[count + lane] = LEAF


def fetched(codes, codes_s, sem):
    fetch = pltpu.make_async_copy(codes, codes_s, sem.at[0])
    fetch.start()
    return fetch


def front_kernel(pos, stren, cores, near, counts, own, edge, near_v, counts_v, acc,
                 gathered, sems, left, right, even, odd, stage, centres, table, targets, codes, codes_s, sem):
    copies = []
    for k in range(FIELDS):
        ref, base = ((pos, k), (stren, k - 3), (cores, 0))[min(k // 3, 2)]
        copies.append((ref.at[pl.ds(base * LEAF, EDGE)], edge.at[pl.ds(k * EDGE, EDGE)]))
    copies += [
        (pos, own.at[pl.ds(0, 96)]),
        (stren, own.at[pl.ds(96, 96)]),
        (cores, own.at[pl.ds(192, 32)]),
        (near, near_v),
        (counts, counts_v),
    ]
    copies = [pltpu.make_async_copy(a, b, sems.at[n]) for n, (a, b) in enumerate(copies)]
    for copy in copies:
        copy.start()
    acc[...] = jnp.zeros_like(acc)
    for copy in copies:
        copy.wait()

    @pl.when(lax.axis_index("bit") & 7 < 3)
    def _():
        found = slot_codes(near_v[...], counts_v[...])
        leaves = early_leaves(found)

        @pl.when(leaves > 0)
        def _():
            codes[...] = jnp.where(early_codes(found, leaves), found, 0)
            fetch = fetched(codes, codes_s, sem)
            build_targets(own, centres, table, stage)
            fetch.wait()
            count = scan(leaves, codes_s, own, centres, gathered, targets, None)
            features(count, gathered, left, right)
            sum_pairs(count, targets, table, left, right, acc, (even, odd))


def local_kernel(near, counts, own, remote, acc, centres, table,
                 gathered, left, right, even, odd, stage, targets, codes, codes_s, sem):
    found = slot_codes(near[...], counts[...])
    codes[...] = found

    @pl.when(lax.axis_index("bit") & 7 < 3)
    def _():
        codes[...] = jnp.where(early_codes(found, early_leaves(found)), 0, found)

    fetch = fetched(codes, codes_s, sem)
    build_targets(own, centres, table, stage)
    acc[...] = jnp.zeros_like(acc)
    fetch.wait()
    count = scan(LEAF, codes_s, own, centres, gathered, targets, remote)
    features(count, gathered, left, right)
    sum_pairs(count, targets, table, left, right, acc, (even, odd))


def remote_kernel(remote, own, centres, table, acc0, acc1, far, p8, p1, p16, p2, p4, outer_part, inner_part,
                  velocity, stretching, far_v, sem, gathered, left, right, even, odd, targets, acc):
    parts = (inner_part, outer_part, p1, p2, p4, p8, p16)
    copy = pltpu.make_async_copy(far, far_v, sem.at[0])
    copy.start()
    acc[...] = jnp.zeros_like(acc)
    count = remote[PAIRS + 7]

    def four(step, _):
        found = []
        for code in [remote[step * 4 + lane] for lane in range(4)]:
            target = (code >> 6) & (LEAF - 1)
            where = pl.ds(code >> 14, FIELDS, stride=EDGE)
            part = (code >> 11) & 7
            source = parts[0][where, :]
            for k in range(1, 7):
                source = jnp.where(part == k, parts[k][where, :], source)
            centre = centres[pl.ds(pl.multiple_of(target * 8, 8), 8), :][:FIELDS]
            found.append((target, scaled(source, centre, code)))
        for lane, (target, source) in enumerate(found):
            n = step * 4 + lane
            gathered[pl.ds(pl.multiple_of(n * 8, 8), FIELDS), :] = source
            targets[n] = target
        return 0

    lax.fori_loop(0, (count + 3) // 4, four, 0)
    close_list(targets, count)
    features(count, gathered, left, right)
    sum_pairs(count, targets, table, left, right, acc, (even, odd))
    copy.wait()

    coefs = far_v[...].T
    for group in range(LEAF // 8):
        rows = pl.ds(group * 8, 8)
        _, off = offsets(own, group)
        a = leaf_fields(own, group, range(3, 6))

        def summed(field, side):
            first = side * SUMS + group * 128 + field
            parts = [
                ref[pl.ds(first + low, 8, stride=16), :] for ref in (acc0, acc1, acc) for low in (0, 6)
            ]
            return (parts[0] + parts[1]) + (parts[2] + parts[3]) + (parts[4] + parts[5])

        ka = [summed(k, 0) for k in range(3)]
        kc = [summed(3 + k, 0) for k in range(3)]
        wa = [summed(k, 1) for k in range(3)]
        wc = [summed(3 + k, 1) for k in range(3)]
        coef = [coefs[group * 8 : group * 8 + 8, k : k + 1] for k in range(12)]
        for i in range(3):
            j, k = (i + 1) % 3, (i + 2) % 3
            near_vel = off[j] * ka[k] - off[k] * ka[j] - kc[i]
            steep = off[j] * wa[k] - off[k] * wa[j] - wc[i]
            near_str = a[j] * ka[k] - a[k] * ka[j] - 3.0 * steep
            grad = [coef[3 + 3 * i + m] for m in range(3)]
            velocity[i, rows, :] = (
                -inv_four_pi * near_vel + coef[i]
                + grad[0] * off[0] + grad[1] * off[1] + grad[2] * off[2]
            )
            stretching[i, rows, :] = (
                -inv_four_pi * near_str + grad[0] * a[0] + grad[1] * a[1] + grad[2] * a[2]
            )


VM = pl.BlockSpec(memory_space=pltpu.VMEM)
SM = pl.BlockSpec(memory_space=pltpu.SMEM)
HB = pl.BlockSpec(memory_space=pltpu.HBM)
PARAMS = pltpu.CompilerParams(vmem_limit_bytes=24 * 2**20)


def body(positions, strengths, cores, far_coef, near_list, near_count):
    bits, sects = lax.axis_size("bit"), lax.axis_size("sect")
    shape = jax.ShapeDtypeStruct
    source_room = [pltpu.VMEM((ROOM * 16, PART), f32), pltpu.VMEM((ROOM * 16, PART), f32)]
    pair_room = source_room + [pltpu.VMEM((HALF, PART, 2 * PART), f32)] * 2
    stage_room = pltpu.VMEM((2048, PART), f32)
    target_room = [pltpu.VMEM((LEAF * 8, PART), f32), pltpu.VMEM((2 * TABLE, PART), bf16)]
    list_room = [
        pltpu.SMEM((ROOM,), i32),
        pltpu.VMEM((SLOTS, LEAF), i32),
        pltpu.SMEM((SLOTS, LEAF), i32),
        pltpu.SemaphoreType.DMA((1,)),
    ]
    gather_room = pltpu.VMEM((ROOM * 8, PART), f32)
    sums = (2 * SUMS, PART)
    fixed = [
        pltpu.with_memory_space_constraint(v, pltpu.HBM)
        for v in (
            positions.reshape(3 * LEAF, PART),
            strengths.reshape(3 * LEAF, PART),
            cores,
            near_list.T,
            near_count.reshape(1, LEAF),
            far_coef,
        )
    ]
    own, edge, near, counts, acc0 = pl.pallas_call(
        front_kernel,
        out_shape=[
            shape((LEAF * FIELDS, PART), f32),
            shape((MOVED, PART), f32),
            shape((SLOTS, LEAF), i32),
            shape((1, LEAF), i32),
            shape(sums, f32),
        ],
        in_specs=[HB] * 5,
        out_specs=[VM] * 5,
        scratch_shapes=[gather_room, pltpu.SemaphoreType.DMA((12,))] + pair_room + [stage_room]
        + target_room + list_room,
        compiler_params=PARAMS,
        name="front",
    )(*fixed[:5])
    moved = [lax.ppermute(edge, "bit", [(i, i ^ (1 << n)) for i in range(bits)]) for n in (0, 3, 4, 1, 2)]
    beside = {i: i + 1 for i in range(1, sects - 1, 2)}
    beside.update({j: i for i, j in beside.items()})
    pairs = [
        (b * sects + i, b * sects + beside[i] if i in beside else (b ^ 1) * sects + i)
        for b in range(bits) for i in range(sects)
    ]
    moved.append(lax.ppermute(edge, ("bit", "sect"), pairs))
    moved.append(lax.ppermute(edge, "sect", [(i, i ^ 1) for i in range(sects)]))
    z1, y1, y2, z2, z4, outer, inner = moved
    remote, acc1, centres, table = pl.pallas_call(
        local_kernel,
        out_shape=[
            shape((PAIRS + 8,), i32),
            shape(sums, f32),
            shape((LEAF * 8, PART), f32),
            shape((2 * TABLE, PART), bf16),
        ],
        in_specs=[VM] * 3,
        out_specs=[SM] + [VM] * 3,
        scratch_shapes=[gather_room] + pair_room + [stage_room] + list_room,
        compiler_params=PARAMS,
        name="local_pairs",
    )(near, counts, own)
    return pl.pallas_call(
        remote_kernel,
        out_shape=[shape((3, LEAF, PART), f32)] * 2,
        in_specs=[SM] + [VM] * 5 + [HB] + [VM] * 7,
        out_specs=[VM, VM],
        scratch_shapes=[pltpu.VMEM((12, LEAF), f32), pltpu.SemaphoreType.DMA((1,)), gather_room] + pair_room
        + [list_room[0], pltpu.VMEM(sums, f32)],
        compiler_params=PARAMS,
        name="remote_pairs",
    )(remote, own, centres, table, acc0, acc1, fixed[5], y1, z1, y2, z2, z4, outer, inner)


def solution(mesh):
    in_specs = (
        P(None, ("bit", "sect"), None),
        P(None, ("bit", "sect"), None),
        P(("bit", "sect"), None),
        P(None, ("bit", "sect")),
        P(("bit", "sect"), None),
        P(("bit", "sect")),
    )
    out_specs = (P(None, ("bit", "sect"), None), P(None, ("bit", "sect"), None))
    return jax.shard_map(body, mesh=mesh, in_specs=in_specs, out_specs=out_specs, check_vma=False)
```

```python
import math

import jax
import jax.numpy as jnp
from jax import lax
from jax.experimental import pallas as pl
from jax.experimental.pallas import tpu as pltpu
from jax.sharding import PartitionSpec as P

inv_four_pi = 1.0 / (4.0 * math.pi)
f32, bf16, i32 = jnp.float32, jnp.bfloat16, jnp.int32

LEAF = 32
PART = 128
SLOTS = 8
EDGE = 24
FIELDS = 7
MOVED = FIELDS * EDGE
PAIRS = LEAF * SLOTS
BATCH = 20
HALF = BATCH // 2
ROOM = PAIRS + 2 * BATCH
TABLE = (LEAF + 1) * 32
SUMS = (LEAF + 1) * 16


def rounded(value):
    return value.astype(bf16).astype(f32)


def split3(value):
    high = rounded(value)
    rest = value - high
    mid = rounded(rest)
    return high, mid, rest - mid


def split2(value):
    high = value.astype(bf16)
    return high, (value - high.astype(f32)).astype(bf16)


def leaf_fields(own, group, fields):
    return [own[pl.ds(k * LEAF + group * 8, 8), :] for k in fields]


def offsets(own, group):
    point = leaf_fields(own, group, range(3))
    centre = [jnp.mean(v, axis=1, keepdims=True) for v in point]
    return centre, [v - c for v, c in zip(point, centre)]


def build_targets(own, centres, table, stage):
    for group in range(LEAF // 8):
        centre, off = offsets(own, group)
        a = leaf_fields(own, group, range(3, 6))
        zero = jnp.zeros((8, PART), f32)
        one = jnp.ones((8, PART), f32)
        for k in range(8):
            row = jnp.broadcast_to(centre[k], (8, PART)) if k < 3 else zero
            centres[pl.ds(group * 64 + k, 8, stride=8), :] = row
        left = [split3(-2.0 * v) for v in off]
        right = [split3(-v) for v in a]
        square = split3(off[0] * off[0] + off[1] * off[1] + off[2] * off[2])
        along = split3(off[0] * a[0] + off[1] * a[1] + off[2] * a[2])
        rows = []
        level = [[(left[k][part], right[k][part]) for k in range(3)] for part in range(3)]
        rows += level[0] * 2 + [(one, zero)] * 2
        rows += level[0] + [(one, zero)] + [(square[k], along[k]) for k in range(3)] + [(zero, zero)]
        rows += level[1] * 2 + [(zero, zero)] * 2
        rows += level[2] * 2 + [(zero, zero)] * 2
        for k, (spread_row, proj_row) in enumerate(rows):
            stage[pl.ds(group * 512 + k, 8, stride=32), :] = spread_row
            stage[pl.ds(group * 512 + 256 + k, 8, stride=32), :] = proj_row
        for side in range(2):
            table[pl.ds(side * TABLE + group * 256, 256), :] = stage[
                pl.ds(group * 512 + side * 256, 256), :
            ].astype(bf16)


def source_fields(gathered, group):
    first = pl.multiple_of(group * 64, 64)
    return [gathered[pl.ds(first + k, 8, stride=8), :] for k in range(FIELDS)]


def source_rows(q, left, right, group):
    x, a, core = q[:3], q[3:6], q[6]
    part = [split3(v) for v in x]
    size = split3(x[0] * x[0] + x[1] * x[1] + x[2] * x[2] + core * core)
    one = jnp.ones((8, PART), f32)
    rows = [part[k][level] for level in (0, 1) for k in range(3)] + [size[0], size[1]]
    rows += [part[k][2] for k in range(3)] + [size[2]] + [one] * 4
    base = pl.multiple_of(group * 128, 128)
    for k, row in enumerate(rows):
        left[pl.ds(base + k, 8, stride=16), :] = row
    crossed = [
        x[1] * a[2] - x[2] * a[1],
        x[2] * a[0] - x[0] * a[2],
        x[0] * a[1] - x[1] * a[0],
    ]
    for k, row in enumerate(a + crossed):
        high = rounded(row)
        right[pl.ds(base + k, 8, stride=16), :] = high
        right[pl.ds(base + 6 + k, 8, stride=16), :] = row - high


def pair_products(pair, target, table, left):
    rows = left[pl.ds(pl.multiple_of(pair * 16, 16), 16), :]
    lhs = jnp.concatenate([rows, rows[:8], rows[:8]], axis=0).astype(bf16)
    first = pl.multiple_of(target * 32, 32)
    rhs = jnp.concatenate([table[pl.ds(first, 32), :], table[pl.ds(TABLE + first, 32), :]], axis=1)
    return lax.dot_general(lhs, rhs, (((0,), (0,)), ((), ())), preferred_element_type=f32)


def pair_total(pair, both, right):
    spread, proj = both[:, :PART], both[:, PART:]
    root = lax.rsqrt(spread)
    square = root * root
    kernel = root * square
    weight = kernel * square * proj
    k_high, k_low = split2(kernel)
    w_high, w_low = split2(weight)
    pairs = jnp.concatenate(
        [jnp.concatenate([k_high, w_high], axis=1), jnp.concatenate([k_low, w_low], axis=1)], axis=0
    )
    rows = right[pl.ds(pl.multiple_of(pair * 16, 16), 16), :].astype(bf16)
    rows = jnp.concatenate([rows, rows], axis=1)
    return jnp.dot(rows, pairs, preferred_element_type=f32)


def half_batch(begin, now, later, target_of, table, left, right, acc, carry):
    last, total = carry
    results = []
    for lane in range(HALF):
        pair = begin + lane
        if later is not None:
            ahead = pair + HALF
            later[lane] = pair_products(ahead, target_of[ahead], table, left)
        results.append((target_of[pair], pair_total(pair, now[lane], right)))
    for target, value in results:
        total = jnp.where(target == last, total, 0.0) + value
        last = target
        first = pl.multiple_of(target * 16, 16)
        for side in range(2):
            acc[pl.ds(side * SUMS + first, 16), :] = total[:, side * PART : (side + 1) * PART]
    return last, total


def features(count, gathered, left, right):
    def two(step, _):
        groups = (2 * step, 2 * step + 1)
        for group, fields in [(g, source_fields(gathered, g)) for g in groups]:
            source_rows(fields, left, right, group)
        return 0

    lax.fori_loop(0, (count + 15) // 16, two, 0)


def sum_pairs(count, target_of, table, left, right, acc, products):
    even, odd = products
    work = (target_of, table, left, right, acc)
    halves = (count + HALF - 1) // HALF

    @pl.when(count > 0)
    def _():
        for lane in range(HALF):
            even[lane] = pair_products(lane, target_of[lane], table, left)

    def step(s, c):
        c = half_batch(s * BATCH, even, odd, *work, c)
        return half_batch(s * BATCH + HALF, odd, even, *work, c)

    carry = (jnp.int32(-1), jnp.zeros((16, 2 * PART), f32))
    carry = lax.fori_loop(0, halves // 2, step, carry)

    @pl.when(halves & 1 == 1)
    def _():
        half_batch((halves - 1) * HALF, even, None, *work, carry)


def slot_codes(near, counts):
    slot = lax.broadcasted_iota(i32, near.shape, 0)
    used = slot < counts
    times = jnp.ones(near.shape, i32)
    fresh = used
    for d in range(1, SLOTS):
        after = pltpu.roll(near, SLOTS - d, 0)
        times = times + ((after == near) & (slot + d < counts)).astype(i32)
        before = pltpu.roll(near, d, 0)
        fresh = fresh & ~((before == near) & (slot >= d))
    owner = near >> 5
    me = jnp.broadcast_to(near[0:1, 0:1] >> 5, near.shape)
    differs = owner ^ me
    bit = differs >> 3
    part = jnp.where(bit == 0, jnp.where(differs == 1, 0, 1), 2)
    for n in range(1, 5):
        part = jnp.where(bit == 1 << n, 2 + n, part)
    mine = differs == 0
    target = lax.broadcasted_iota(i32, near.shape, 1)
    code = jnp.where(mine, 1, 2) + times * 4 + target * 64 + part * 2048 + (near & (LEAF - 1)) * 16384
    return jnp.where(fresh, code, 0)


def early_leaves(codes):
    z = lax.axis_index("bit") & 7
    local = (codes & 1).astype(f32)
    row = lax.broadcasted_iota(i32, (LEAF, LEAF), 0)
    upto = (row <= lax.broadcasted_iota(i32, (LEAF, LEAF), 1)).astype(f32)
    held = jnp.sum(jnp.dot(local, upto, preferred_element_type=f32), axis=0, keepdims=True)
    count = jnp.sum(local).astype(i32)
    ahead = jnp.minimum(count - 8 * (z + 2) - 16, 80)
    leaves = jnp.sum((held <= ahead.astype(f32)).astype(f32)).astype(i32)
    return jnp.where((z < 3) & (ahead >= 12), leaves, 0)


def early_codes(codes, leaves):
    return (codes & 1 == 1) & (lax.broadcasted_iota(i32, codes.shape, 1) < leaves)


def scaled(source, centre, code):
    row = lax.broadcasted_iota(i32, (FIELDS, PART), 0)
    found = source - centre
    return jnp.where((row >= 3) & (row < 6), found * ((code >> 2) & 15).astype(f32), found)


def scan(leaves, codes, own, centres, gathered, targets, remote):
    def leaf(t, carry):
        place, outside = carry
        centre = centres[pl.ds(pl.multiple_of(t * 8, 8), 8), :][:FIELDS]
        listed = [codes[slot, t] for slot in range(SLOTS)]
        sources = [
            scaled(own[pl.ds(code >> 14, FIELDS, stride=LEAF), :], centre, code) for code in listed
        ]
        for code, source in zip(listed, sources):
            gathered[pl.ds(pl.multiple_of(place * 8, 8), FIELDS), :] = source
            targets[place] = t
            place = place + (code & 1)
            if remote is not None:
                remote[outside] = code
                outside = outside + ((code >> 1) & 1)
        return place, outside

    count, outside = lax.fori_loop(0, leaves, leaf, (jnp.int32(0), jnp.int32(0)))
    if remote is not None:
        for k in range(3):
            remote[outside + k] = 0
        remote[PAIRS + 7] = outside
    close_list(targets, count)
    return count


def close_list(targets, count):
    for lane in range(2 * BATCH):
        targets[count + lane] = LEAF


def fetched(codes, codes_s, sem):
    fetch = pltpu.make_async_copy(codes, codes_s, sem.at[0])
    fetch.start()
    return fetch


def front_kernel(pos, stren, cores, near, counts, own, edge, near_v, counts_v, acc,
                 gathered, sems, left, right, even, odd, stage, centres, table, targets, codes, codes_s, sem):
    copies = []
    for k in range(FIELDS):
        ref, base = ((pos, k), (stren, k - 3), (cores, 0))[min(k // 3, 2)]
        copies.append((ref.at[pl.ds(base * LEAF, EDGE)], edge.at[pl.ds(k * EDGE, EDGE)]))
    copies += [
        (pos, own.at[pl.ds(0, 96)]),
        (stren, own.at[pl.ds(96, 96)]),
        (cores, own.at[pl.ds(192, 32)]),
        (near, near_v),
        (counts, counts_v),
    ]
    copies = [pltpu.make_async_copy(a, b, sems.at[n]) for n, (a, b) in enumerate(copies)]
    for copy in copies:
        copy.start()
    acc[...] = jnp.zeros_like(acc)
    for copy in copies:
        copy.wait()

    @pl.when(lax.axis_index("bit") & 7 < 3)
    def _():
        found = slot_codes(near_v[...], counts_v[...])
        leaves = early_leaves(found)

        @pl.when(leaves > 0)
        def _():
            codes[...] = jnp.where(early_codes(found, leaves), found, 0)
            fetch = fetched(codes, codes_s, sem)
            build_targets(own, centres, table, stage)
            fetch.wait()
            count = scan(leaves, codes_s, own, centres, gathered, targets, None)
            features(count, gathered, left, right)
            sum_pairs(count, targets, table, left, right, acc, (even, odd))


def local_kernel(near, counts, own, remote, acc, centres, table,
                 gathered, left, right, even, odd, stage, targets, codes, codes_s, sem):
    found = slot_codes(near[...], counts[...])
    codes[...] = found

    @pl.when(lax.axis_index("bit") & 7 < 3)
    def _():
        codes[...] = jnp.where(early_codes(found, early_leaves(found)), 0, found)

    fetch = fetched(codes, codes_s, sem)
    build_targets(own, centres, table, stage)
    acc[...] = jnp.zeros_like(acc)
    fetch.wait()
    count = scan(LEAF, codes_s, own, centres, gathered, targets, remote)
    features(count, gathered, left, right)
    sum_pairs(count, targets, table, left, right, acc, (even, odd))


def remote_kernel(remote, own, centres, table, acc0, acc1, far, p1, p8, p16, p2, p4, outer_part, inner_part,
                  velocity, stretching, far_v, sem, gathered, left, right, even, odd, targets, acc):
    parts = (inner_part, outer_part, p1, p2, p4, p8, p16)
    copy = pltpu.make_async_copy(far, far_v, sem.at[0])
    copy.start()
    acc[...] = jnp.zeros_like(acc)
    count = remote[PAIRS + 7]

    def four(step, _):
        found = []
        for code in [remote[step * 4 + lane] for lane in range(4)]:
            target = (code >> 6) & (LEAF - 1)
            where = pl.ds(code >> 14, FIELDS, stride=EDGE)
            part = (code >> 11) & 7
            source = parts[0][where, :]
            for k in range(1, 7):
                source = jnp.where(part == k, parts[k][where, :], source)
            centre = centres[pl.ds(pl.multiple_of(target * 8, 8), 8), :][:FIELDS]
            found.append((target, scaled(source, centre, code)))
        for lane, (target, source) in enumerate(found):
            n = step * 4 + lane
            gathered[pl.ds(pl.multiple_of(n * 8, 8), FIELDS), :] = source
            targets[n] = target
        return 0

    lax.fori_loop(0, (count + 3) // 4, four, 0)
    close_list(targets, count)
    features(count, gathered, left, right)
    sum_pairs(count, targets, table, left, right, acc, (even, odd))
    copy.wait()

    coefs = far_v[...].T
    for group in range(LEAF // 8):
        rows = pl.ds(group * 8, 8)
        _, off = offsets(own, group)
        a = leaf_fields(own, group, range(3, 6))

        def summed(field, side):
            first = side * SUMS + group * 128 + field
            parts = [
                ref[pl.ds(first + low, 8, stride=16), :] for ref in (acc0, acc1, acc) for low in (0, 6)
            ]
            return (parts[0] + parts[1]) + (parts[2] + parts[3]) + (parts[4] + parts[5])

        ka = [summed(k, 0) for k in range(3)]
        kc = [summed(3 + k, 0) for k in range(3)]
        wa = [summed(k, 1) for k in range(3)]
        wc = [summed(3 + k, 1) for k in range(3)]
        coef = [coefs[group * 8 : group * 8 + 8, k : k + 1] for k in range(12)]
        for i in range(3):
            j, k = (i + 1) % 3, (i + 2) % 3
            near_vel = off[j] * ka[k] - off[k] * ka[j] - kc[i]
            steep = off[j] * wa[k] - off[k] * wa[j] - wc[i]
            near_str = a[j] * ka[k] - a[k] * ka[j] - 3.0 * steep
            grad = [coef[3 + 3 * i + m] for m in range(3)]
            velocity[i, rows, :] = (
                -inv_four_pi * near_vel + coef[i]
                + grad[0] * off[0] + grad[1] * off[1] + grad[2] * off[2]
            )
            stretching[i, rows, :] = (
                -inv_four_pi * near_str + grad[0] * a[0] + grad[1] * a[1] + grad[2] * a[2]
            )


VM = pl.BlockSpec(memory_space=pltpu.VMEM)
SM = pl.BlockSpec(memory_space=pltpu.SMEM)
HB = pl.BlockSpec(memory_space=pltpu.HBM)
PARAMS = pltpu.CompilerParams(vmem_limit_bytes=24 * 2**20)


def body(positions, strengths, cores, far_coef, near_list, near_count):
    bits, sects = lax.axis_size("bit"), lax.axis_size("sect")
    shape = jax.ShapeDtypeStruct
    source_room = [pltpu.VMEM((ROOM * 16, PART), f32), pltpu.VMEM((ROOM * 16, PART), f32)]
    pair_room = source_room + [pltpu.VMEM((HALF, PART, 2 * PART), f32)] * 2
    stage_room = pltpu.VMEM((2048, PART), f32)
    target_room = [pltpu.VMEM((LEAF * 8, PART), f32), pltpu.VMEM((2 * TABLE, PART), bf16)]
    list_room = [
        pltpu.SMEM((ROOM,), i32),
        pltpu.VMEM((SLOTS, LEAF), i32),
        pltpu.SMEM((SLOTS, LEAF), i32),
        pltpu.SemaphoreType.DMA((1,)),
    ]
    gather_room = pltpu.VMEM((ROOM * 8, PART), f32)
    sums = (2 * SUMS, PART)
    fixed = [
        pltpu.with_memory_space_constraint(v, pltpu.HBM)
        for v in (
            positions.reshape(3 * LEAF, PART),
            strengths.reshape(3 * LEAF, PART),
            cores,
            near_list.T,
            near_count.reshape(1, LEAF),
            far_coef,
        )
    ]
    own, edge, near, counts, acc0 = pl.pallas_call(
        front_kernel,
        out_shape=[
            shape((LEAF * FIELDS, PART), f32),
            shape((MOVED, PART), f32),
            shape((SLOTS, LEAF), i32),
            shape((1, LEAF), i32),
            shape(sums, f32),
        ],
        in_specs=[HB] * 5,
        out_specs=[VM] * 5,
        scratch_shapes=[gather_room, pltpu.SemaphoreType.DMA((12,))] + pair_room + [stage_room]
        + target_room + list_room,
        compiler_params=PARAMS,
        name="front",
    )(*fixed[:5])
    moved = [lax.ppermute(edge, "bit", [(i, i ^ (1 << n)) for i in range(bits)]) for n in (0, 3, 4, 1, 2)]
    beside = {i: i + 1 for i in range(1, sects - 1, 2)}
    beside.update({j: i for i, j in beside.items()})
    pairs = [
        (b * sects + i, b * sects + beside[i] if i in beside else (b ^ 1) * sects + i)
        for b in range(bits) for i in range(sects)
    ]
    moved.append(lax.ppermute(edge, ("bit", "sect"), pairs))
    moved.append(lax.ppermute(edge, "sect", [(i, i ^ 1) for i in range(sects)]))
    z1, y1, y2, z2, z4, outer, inner = moved
    remote, acc1, centres, table = pl.pallas_call(
        local_kernel,
        out_shape=[
            shape((PAIRS + 8,), i32),
            shape(sums, f32),
            shape((LEAF * 8, PART), f32),
            shape((2 * TABLE, PART), bf16),
        ],
        in_specs=[VM] * 3,
        out_specs=[SM] + [VM] * 3,
        scratch_shapes=[gather_room] + pair_room + [stage_room] + list_room,
        compiler_params=PARAMS,
        name="local_pairs",
    )(near, counts, own)
    return pl.pallas_call(
        remote_kernel,
        out_shape=[shape((3, LEAF, PART), f32)] * 2,
        in_specs=[SM] + [VM] * 5 + [HB] + [VM] * 7,
        out_specs=[VM, VM],
        scratch_shapes=[pltpu.VMEM((12, LEAF), f32), pltpu.SemaphoreType.DMA((1,)), gather_room] + pair_room
        + [list_room[0], pltpu.VMEM(sums, f32)],
        compiler_params=PARAMS,
        name="remote_pairs",
    )(remote, own, centres, table, acc0, acc1, fixed[5], z1, y1, y2, z2, z4, outer, inner)


def solution(mesh):
    in_specs = (
        P(None, ("bit", "sect"), None),
        P(None, ("bit", "sect"), None),
        P(("bit", "sect"), None),
        P(None, ("bit", "sect")),
        P(("bit", "sect"), None),
        P(("bit", "sect")),
    )
    out_specs = (P(None, ("bit", "sect"), None), P(None, ("bit", "sect"), None))
    return jax.shard_map(body, mesh=mesh, in_specs=in_specs, out_specs=out_specs, check_vma=False)
```
